256 devices in a mesh: row: 32 (over z, x_hi, core), col: 8 (over y, x_lo).
Axes of the slice: x: 4 (x_hi: 2, x_lo: 2; x = x_hi * 2 + x_lo), y: 4, z: 8, core: 2. Of those that a mesh axis runs over, the one named last changes fastest.
Arguments:
- tokens: bfloat16 [512, 128, 1024], P('row', 'col'), may hold values from -6 to 6
- grad_out: bfloat16 [512, 128, 1024], P('row', 'col'), may hold values from -6 to 6
- w_qkv: bfloat16 [1024, 3072], replicated, may hold values from -1 to 1
- w_proj: bfloat16 [1024, 1024], replicated, may hold values from -0.1875 to 0.1875
- norm_gain: float32 [1024], replicated, may hold values from 0.1 to 1.9
- logit_scale: float32 [32], replicated, may hold values from 5 to 128
Outputs:
- grad_tokens: bfloat16 [512, 128, 1024], P('row', 'col')
- grad_wvalue: float32 [1024, 1024], P(('row', 'col'))
- grad_wproj: float32 [1024, 1024], P(('row', 'col'))
The draws below stay inside these ranges and needn't reach their ends.
All inputs are finite; a program needn't handle non-finite values.
Results may differ from the reference program's by a relative error of at most 0.018.
The reference program's roundings to bfloat16 on the way (of `probs_bf`, `attended_bf`, `grad_mix_bf`, `grad_att_bf`, `grad_score_bf`, `grad_qkv_bf` and `grad_input_bf`) count: a program that leaves them out, or rounds other values in their place, can miss the bound.
Values may be sent and summed in bfloat16 or wider, within the bound.
No kernel may reach another device: no remote copies, remote signals or barrier semaphores. Data moves between devices by JAX's collectives and lax.ppermute only.
A program may use at most 128 MiB of HBM per device.

```python
import math
import jax
import jax.numpy as jnp
from jax import lax

C = 1024
HEADS = 32
WIN = 16
GH = 512
GW = 128


def draw_tokens(key, part):
    key = jax.random.fold_in(key, 7)
    noise = jax.random.normal(key, (GH, GW, C), jnp.float32)
    values = noise
    return jnp.clip(values, -6.0, 6.0).astype(jnp.bfloat16)


def draw_w_qkv(key, part):
    key = jax.random.fold_in(key, 11)
    weights = jnp.clip(jax.random.normal(key, (C, 3 * C), jnp.float32), -6.0, 6.0) * C ** (-0.5)
    return jnp.clip(weights, -1.0, 1.0).astype(jnp.bfloat16)


def draw_logit_scale(key, part):
    key = jax.random.fold_in(key, 13)
    first = jax.random.fold_in(key, 0)
    spread = jnp.exp(jax.random.uniform(first, (HEADS,), jnp.float32, math.log(5.0), math.log(128.0)))
    return jnp.clip(spread, 5.0, 128.0).astype(jnp.float32)


def levels(stream_key, dims, cuts, smallest, high):
    def one(position, blocks):
        steps = jax.random.uniform(jax.random.fold_in(jax.random.fold_in(stream_key, 6), position), (blocks,), jnp.float32, smallest / len(cuts), high / len(cuts))
        return jnp.repeat(jnp.exp(steps), dims[position] // blocks).reshape((-1,) + (1,) * (len(dims) - position - 1))

    level = one(*cuts[0])
    for cut in cuts[1:]:
        level = level * one(*cut)
    return level


def scatter_about(rng, dims, scale, most, cuts=(), kind=jnp.bfloat16):
    loudness = levels(rng, dims, cuts, -0.22, 0.18) if cuts else 1.0
    values = jax.random.normal(rng, dims, jnp.float32) * scale * loudness
    return jnp.minimum(jnp.maximum(values, -most), most).astype(kind)


def setup_inputs(seed: int = 0) -> dict:
    streams_of = jax.random.split(jax.random.key(seed), 7)
    tokens = draw_tokens(jax.random.fold_in(streams_of[6], 71), 0)
    grad_out = scatter_about(streams_of[1], (GH, GW, C), 1.0, 6.0, ((0, 32), (1, 8)))
    w_qkv = draw_w_qkv(jax.random.fold_in(streams_of[6], 71), 0)
    w_proj = scatter_about(streams_of[3], (C, C), C ** -0.5, 0.1875)
    norm_gain = jnp.clip(1.0 + 0.18 * jax.random.normal(streams_of[4], (C,), jnp.float32), 0.1, 1.9)
    logit_scale = draw_logit_scale(jax.random.fold_in(streams_of[6], 71), 0)
    return dict(tokens=tokens, grad_out=grad_out, w_qkv=w_qkv, w_proj=w_proj, norm_gain=norm_gain, logit_scale=logit_scale)


EPS_NORM = 1e-06
EPS_LN = 1e-05
HIGHEST = lax.Precision.HIGHEST

def as_float(array):
    return array.astype(jnp.float32)

def mixed_einsum(form, left, right):
    return jnp.einsum(form, as_float(left), as_float(right), precision=HIGHEST)

def window_grads(s_win, g_win, label, w_qkv, w_proj, norm_gain, logit_scale):
    width = w_qkv.shape[0]
    tokens_win = s_win.shape[0]
    head_dim = width // HEADS
    projected = jnp.dot(s_win, w_qkv, preferred_element_type=jnp.float32)
    query_raw = projected[:, :width].reshape(tokens_win, HEADS, head_dim)
    key_raw = projected[:, width:2 * width].reshape(tokens_win, HEADS, head_dim)
    value_raw = projected[:, 2 * width:].reshape(tokens_win, HEADS, head_dim)
    query_scale = lax.rsqrt(lax.optimization_barrier(jnp.sum(query_raw * query_raw, axis=-1, keepdims=True)) + EPS_NORM)
    key_scale = lax.rsqrt(lax.optimization_barrier(jnp.sum(key_raw * key_raw, axis=-1, keepdims=True)) + EPS_NORM)
    query_unit = query_raw * query_scale
    key_unit = key_raw * key_scale
    query_bf = query_unit.astype(jnp.bfloat16)
    key_bf = key_unit.astype(jnp.bfloat16)
    value_bf = value_raw.astype(jnp.bfloat16)
    same = (label[:, None] == label[None, :])[None]
    scales = logit_scale[:, None, None]
    logits = scales * mixed_einsum('qhd,khd->hqk', query_bf, key_bf)
    logits = jnp.where(same, logits, jnp.float32(-1000000000.0))
    top = lax.optimization_barrier(jnp.max(logits, axis=-1, keepdims=True))
    expo = jnp.exp(logits - top)
    probs = expo / lax.optimization_barrier(jnp.sum(expo, axis=-1, keepdims=True))
    probs_bf = probs.astype(jnp.bfloat16)
    attended = mixed_einsum('hqk,khd->qhd', probs_bf, value_bf)
    attended_bf = attended.reshape(tokens_win, width).astype(jnp.bfloat16)
    mixed = jnp.dot(attended_bf, w_proj, preferred_element_type=jnp.float32)
    center = mixed - lax.optimization_barrier(jnp.mean(mixed, axis=-1, keepdims=True))
    inv_std = lax.rsqrt(lax.optimization_barrier(jnp.mean(center * center, axis=-1, keepdims=True)) + EPS_LN)
    normed = center * inv_std
    grad_y = as_float(g_win)
    grad_norm = grad_y * norm_gain[None, :]
    grad_mix = inv_std * (grad_norm - lax.optimization_barrier(jnp.mean(grad_norm, axis=-1, keepdims=True)) - normed * lax.optimization_barrier(jnp.mean(grad_norm * normed, axis=-1, keepdims=True)))
    grad_mix_bf = grad_mix.astype(jnp.bfloat16)
    proj_term = jnp.dot(attended_bf.T, grad_mix_bf, preferred_element_type=jnp.float32)
    grad_att_bf = jnp.dot(grad_mix_bf, w_proj.T, preferred_element_type=jnp.float32).astype(jnp.bfloat16)
    grad_att_heads = grad_att_bf.reshape(tokens_win, HEADS, head_dim)
    grad_value = mixed_einsum('hqk,qhd->khd', probs_bf, grad_att_heads)
    grad_prob = mixed_einsum('qhd,khd->hqk', grad_att_heads, value_bf)
    grad_score = probs * (grad_prob - lax.optimization_barrier(jnp.sum(grad_prob * probs, axis=-1, keepdims=True)))
    grad_score_bf = (scales * grad_score).astype(jnp.bfloat16)
    grad_qunit = mixed_einsum('hqk,khd->qhd', grad_score_bf, key_bf)
    grad_kunit = mixed_einsum('hqk,qhd->khd', grad_score_bf, query_bf)
    grad_query = query_scale * (grad_qunit - query_unit * lax.optimization_barrier(jnp.sum(grad_qunit * query_unit, axis=-1, keepdims=True)))
    grad_key = key_scale * (grad_kunit - key_unit * lax.optimization_barrier(jnp.sum(grad_kunit * key_unit, axis=-1, keepdims=True)))
    grad_qkv_bf = jnp.concatenate([grad_query.reshape(tokens_win, width), grad_key.reshape(tokens_win, width), grad_value.reshape(tokens_win, width)], axis=1).astype(jnp.bfloat16)
    value_term = jnp.dot(s_win.T, grad_qkv_bf[:, 2 * width:], preferred_element_type=jnp.float32)
    grad_input_bf = jnp.dot(grad_qkv_bf, w_qkv.T, preferred_element_type=jnp.float32).astype(jnp.bfloat16)
    return (grad_input_bf, value_term, proj_term)

def reference(tokens, grad_out, w_qkv, w_proj, norm_gain, logit_scale):
    half_win = WIN // 2
    width = tokens.shape[2]
    win_rows = GH // WIN
    win_cols = GW // WIN
    shifted = jnp.roll(tokens, (-half_win, -half_win), axis=(0, 1))
    grad_shift = jnp.roll(grad_out, (-half_win, -half_win), axis=(0, 1))
    row_ids = jnp.arange(GH, dtype=jnp.int32)
    col_ids = jnp.arange(GW, dtype=jnp.int32)
    row_label = jnp.where(row_ids < GH - WIN, 0, jnp.where(row_ids < GH - half_win, 1, 2)).astype(jnp.int32)
    col_label = jnp.where(col_ids < GW - WIN, 0, jnp.where(col_ids < GW - half_win, 1, 2)).astype(jnp.int32)
    labels = (3 * row_label[:, None] + col_label[None, :])[:, :, None]

    def windows(array):
        depth = array.shape[2]
        split = array.reshape(win_rows, WIN, win_cols, WIN, depth).transpose(0, 2, 1, 3, 4)
        return split.reshape(win_rows * win_cols, WIN * WIN, depth)

    def step(carry, item):
        s_win, g_win, label = item
        grad_input_bf, value_term, proj_term = window_grads(s_win, g_win, label[:, 0], w_qkv, w_proj, norm_gain, logit_scale)
        return ((carry[0] + value_term, carry[1] + proj_term), grad_input_bf)
    start = (jnp.zeros((width, width), jnp.float32), jnp.zeros((width, width), jnp.float32))
    sums, stacked = lax.scan(step, start, (windows(shifted), windows(grad_shift), windows(labels)))
    grid = stacked.reshape(win_rows, win_cols, WIN, WIN, width).transpose(0, 2, 1, 3, 4).reshape(GH, GW, width)
    back = jnp.roll(grid, (half_win, half_win), axis=(0, 1))
    grad_tokens = (as_float(grad_out) + as_float(back)).astype(jnp.bfloat16)
    return (grad_tokens, sums[0], sums[1])
```

```python
import functools
import math

import jax
import jax.numpy as jnp
from jax import lax
from jax.experimental import pallas as pl
from jax.experimental.pallas import tpu as pltpu
from jax.sharding import PartitionSpec as P

HEADS = 32
WIN = 16
HALF = WIN // 2
DIM = 32
TOK = WIN * WIN
C = 1024
EPS_NORM = 1e-06
EPS_LN = 1e-05
LOG2E = math.log2(math.e)
BLOCK = 2.0**20
BF = jnp.bfloat16
F32 = jnp.float32
MIB = 2**20


def dot(left, right, dims=((1,), (0,))):
    return lax.dot_general(left, right, (dims, ((), ())), preferred_element_type=F32)


TN = ((0,), (0,))
NT = ((1,), (1,))
TT = ((0,), (1,))
STEP = 8


def head_rows(h):
    return pl.ds(pl.multiple_of(h * DIM, DIM), DIM)


def last_window(rows, cols):
    last_row = (lax.axis_index("row") == rows - 1).astype(F32)
    last_col = (lax.axis_index("col") == cols - 1).astype(F32)
    return last_row, last_col


def mask_features(last_row, last_col):
    feature = lax.broadcasted_iota(jnp.int32, (16, TOK), 0)
    token = lax.broadcasted_iota(jnp.int32, (16, TOK), 1)
    low = (token // (TOK // 2)).astype(F32)
    far = (token // (TOK // 4) % 2).astype(F32)

    def rows(*values):
        out = jnp.zeros((16, TOK), F32)
        for n, value in enumerate(values):
            out = jnp.where(feature == n, value, out)
        return out

    key = rows(low, 1 - low, far, 1 - far)
    query = -BLOCK * rows(
        last_row * (1 - low), last_row * low, last_col * (1 - far), last_col * far
    )
    return key.astype(BF), query.astype(BF)


def attention_kernel(
    rows, cols, x0_ref, x1_ref, x2_ref, x3_ref, w_hbm_ref, scale_ref,
    att_ref, probs_ref, query_ref, key_ref, value_ref, unit_scale_ref, w_qkv_ref, sems,
):
    copies = []
    for n in range(3):
        span = pl.ds(n * C, C)
        copies.append(
            pltpu.make_async_copy(w_hbm_ref.at[:, span], w_qkv_ref.at[:, span], sems.at[n])
        )
        copies[-1].start()
    key_mask, query_mask = mask_features(*last_window(rows, cols))
    x = jnp.concatenate([x0_ref[...], x1_ref[...], x2_ref[...], x3_ref[...]], axis=0)
    for col in range(0, 3 * C, TOK):
        if col % C == 0:
            copies[col // C].wait()
        raw = dot(x, w_qkv_ref[:, col : col + TOK]).T
        if col < 2 * C:
            heads = raw.reshape(TOK // DIM, DIM, TOK)
            inv = lax.rsqrt(jnp.sum(heads * heads, axis=1, keepdims=True) + EPS_NORM)
            unit = (heads * inv).reshape(TOK, TOK)
            unit_scale_ref[col // DIM : (col + TOK) // DIM, :] = inv[:, 0, :]
            if col < C:
                query_ref[col : col + TOK, :] = unit
            else:
                key_ref[col - C : col - C + TOK, :] = unit
        else:
            value_ref[col - 2 * C : col - 2 * C + TOK, :] = raw.astype(BF)

    def head(h, carry):
        rows = head_rows(h)
        raw = dot(
            jnp.concatenate([key_ref[rows, :].astype(BF), key_mask], axis=0),
            jnp.concatenate([query_ref[rows, :].astype(BF), query_mask], axis=0),
            TN,
        )
        top = jnp.max(raw, axis=0, keepdims=True)
        expo = jnp.exp2((raw - top) * (scale_ref[h] * LOG2E))
        probs = expo * (1.0 / jnp.sum(expo, axis=0, keepdims=True))
        probs_ref[h] = probs
        att_ref[rows, :] = dot(probs.astype(BF), value_ref[rows, :], TT).T.astype(BF)
        return carry

    lax.fori_loop(0, HEADS, head, 0, unroll=8)


def norm_kernel(
    att_ref, g0_ref, g1_ref, g2_ref, g3_ref, order_ref, w_proj_ref, gain_ref,
    near_ref, far_ref, grad_att_ref,
):
    g = jnp.concatenate([g0_ref[...], g1_ref[...], g2_ref[...], g3_ref[...]], axis=0)
    mixed = dot(att_ref[...], w_proj_ref[...], TN)
    center = mixed - jnp.mean(mixed, axis=-1, keepdims=True)
    inv_std = lax.rsqrt(jnp.mean(center * center, axis=-1, keepdims=True) + EPS_LN)
    normed = center * inv_std
    grad_norm = g.astype(F32) * gain_ref[...]
    grad_mix = inv_std * (
        grad_norm
        - jnp.mean(grad_norm, axis=-1, keepdims=True)
        - normed * jnp.mean(grad_norm * normed, axis=-1, keepdims=True)
    )
    grad_mix = grad_mix.astype(BF)
    for row in range(0, C, TOK):
        att = dot(order_ref[row : row + TOK, :], att_ref[...]).astype(BF)
        out_ref = near_ref if row < C // 2 else far_ref
        out_ref[row % (C // 2) : row % (C // 2) + TOK, :] = dot(att, grad_mix).astype(BF)
    for row in range(0, C, TOK):
        grad_att_ref[row : row + TOK, :] = dot(
            w_proj_ref[row : row + TOK, :], grad_mix, NT
        ).astype(BF)


def value_kernel(
    x0_ref, x1_ref, x2_ref, x3_ref, order_ref, probs_ref, grad_att_ref,
    near_ref, far_ref, grad_value_ref,
):
    tokens = jnp.concatenate([x0_ref[...], x1_ref[...], x2_ref[...], x3_ref[...]], axis=0)

    def head(h, carry):
        rows = head_rows(h)
        grad_value_ref[rows, :] = dot(
            grad_att_ref[rows, :], probs_ref[h].astype(BF), NT
        ).astype(BF)
        return carry

    lax.fori_loop(0, HEADS, head, 0, unroll=8)
    grad_value = grad_value_ref[...]
    for row in range(0, C, TOK):
        x = dot(order_ref[row : row + TOK, :], tokens, NT).astype(BF)
        out_ref = near_ref if row < C // 2 else far_ref
        out_ref[row % (C // 2) : row % (C // 2) + TOK, :] = dot(x, grad_value, NT).astype(BF)


def score_kernel(
    probs_ref, grad_att_ref, query_ref, key_ref, value_ref, q_scale_ref, k_scale_ref,
    scale_ref, after_ref, grad_query_ref, grad_key_ref, grad_score_ref,
):
    first = pl.program_id(0) * STEP

    def scores(n, carry):
        rows = head_rows(n)
        probs = probs_ref[n]
        grad_prob = dot(value_ref[rows, :], grad_att_ref[rows, :], TN)
        mean = jnp.sum(grad_prob * probs, axis=0, keepdims=True)
        grad_score_ref[n] = (scale_ref[first + n] * (probs * (grad_prob - mean))).astype(BF)
        return carry

    def units(n, carry):
        rows = head_rows(n)
        query = query_ref[rows, :]
        key = key_ref[rows, :]
        grad_score = grad_score_ref[n]
        grad_query = dot(key.astype(BF), grad_score)
        grad_key = dot(grad_score, query.astype(BF), NT).T
        grad_query = q_scale_ref[pl.ds(n, 1), :] * (
            grad_query - query * jnp.sum(grad_query * query, axis=0, keepdims=True)
        )
        grad_key = k_scale_ref[pl.ds(n, 1), :] * (
            grad_key - key * jnp.sum(grad_key * key, axis=0, keepdims=True)
        )
        grad_query_ref[rows, :] = grad_query.astype(BF)
        grad_key_ref[rows, :] = grad_key.astype(BF)
        return carry

    lax.fori_loop(0, STEP, scores, 0, unroll=STEP)
    lax.fori_loop(0, STEP, units, 0, unroll=STEP)


def input_kernel(*refs):
    parts, w_qkv_ref, out_refs = refs[:-5], refs[-5], refs[-4:]
    for row in range(0, C, TOK):
        total, col = 0.0, 0
        for part in parts:
            size = part.shape[0]
            total += dot(w_qkv_ref[row : row + TOK, col : col + size], part[...])
            col += size
        total = total.T.astype(BF)
        for n, out_ref in enumerate(out_refs):
            out_ref[:, row : row + TOK] = total[n * 64 : n * 64 + 64]


VM = pl.BlockSpec(memory_space=pltpu.VMEM)
SM = pl.BlockSpec(memory_space=pltpu.SMEM)


def shape(dims, kind):
    return jax.ShapeDtypeStruct(dims, kind)


def call(kernel, outs, ins, micros, name, limit, scratch=()):
    return pl.pallas_call(
        kernel,
        out_shape=outs,
        in_specs=ins,
        out_specs=jax.tree.map(lambda _: VM, outs),
        scratch_shapes=scratch,
        compiler_params=pltpu.CompilerParams(vmem_limit_bytes=limit * MIB),
        cost_estimate=pl.CostEstimate(
            flops=int(micros * 11 * 10**8), bytes_accessed=MIB, transcendentals=0
        ),
        name=name,
    )


def attention(quads, w_qkv, scale, rows, cols):
    flat = shape((C, TOK), F32)
    flat_bf = shape((C, TOK), BF)
    outs = (
        flat_bf, shape((HEADS, TOK, TOK), F32), flat, flat, flat_bf, shape((2 * HEADS, TOK), F32),
    )
    kernel = functools.partial(attention_kernel, rows, cols)
    scratch = [pltpu.VMEM((C, 3 * C), BF), pltpu.SemaphoreType.DMA((3,))]
    return call(
        kernel, outs, [VM] * 4 + [pl.BlockSpec(memory_space=pltpu.HBM), SM], 14,
        "attention_part", 24, scratch,
    )(*quads, pltpu.with_memory_space_constraint(w_qkv, pltpu.HBM), scale)


def output_norm(att, quads, order, w_proj, gain):
    half = shape((C // 2, C), BF)
    return call(norm_kernel, (half, half, shape((C, TOK), BF)), [VM] * 8, 3, "norm_part", 24)(
        att, *quads, order, w_proj, gain
    )


def value_grads(quads, order, probs, grad_att):
    half = shape((C // 2, C), BF)
    return call(value_kernel, (half, half, shape((C, TOK), BF)), [VM] * 7, 4, "value_part", 24)(
        *quads, order, probs, grad_att
    )


def score_grads(probs, grad_att, query, key, value, unit_scale, scale, after):
    wide = pl.BlockSpec((STEP * DIM, TOK), lambda n: (n, 0))
    steps = HEADS // STEP
    streamed = [
        pltpu.with_memory_space_constraint(array, pltpu.HBM)
        for array in (probs, grad_att, query, key, value)
    ]
    return pl.pallas_call(
        score_kernel,
        out_shape=(shape((C, TOK), BF),) * 2,
        grid=(steps,),
        in_specs=[
            pl.BlockSpec((STEP, TOK, TOK), lambda n: (n, 0, 0)),
            wide,
            wide,
            wide,
            wide,
            pl.BlockSpec((STEP, TOK), lambda n: (n, 0)),
            pl.BlockSpec((STEP, TOK), lambda n: (n + steps, 0)),
            SM,
            pl.BlockSpec(memory_space=pl.ANY),
        ],
        out_specs=(wide, wide),
        scratch_shapes=[pltpu.VMEM((STEP, TOK, TOK), BF)],
        compiler_params=pltpu.CompilerParams(vmem_limit_bytes=24 * MIB),
        cost_estimate=pl.CostEstimate(flops=10**8, bytes_accessed=MIB, transcendentals=0),
        name="score_part",
    )(*streamed, unit_scale, unit_scale, scale, after)


def input_grad(parts, w_qkv):
    outs = (shape((TOK // 4, C), BF),) * 4
    return call(input_kernel, outs, [VM] * (len(parts) + 1), 0.2, "input_part", 24)(*parts, w_qkv)


def passed(array, d_row, d_col, rows, cols):
    pairs = [
        (r * cols + c, (r + d_row) % rows * cols + (c + d_col) % cols)
        for r in range(rows)
        for c in range(cols)
    ]
    return lax.ppermute(array, ("row", "col"), pairs)


def window(array, rows, cols):
    def quad(r, c):
        return array[r : r + HALF, c : c + HALF].reshape(TOK // 4, C)

    return (
        quad(HALF, HALF),
        passed(quad(HALF, 0), 0, -1, rows, cols),
        passed(quad(0, HALF), -1, 0, rows, cols),
        passed(quad(0, 0), -1, -1, rows, cols),
    )


def line(x, y, z, core):
    return ((z * 2 + x // 2) * 2 + core) * 8 + y * 2 + x % 2


CHIPS = [(x, y, z, core) for x in range(4) for y in range(4) for z in range(8) for core in range(2)]
BOTH = ("row", "col")


def other_core(array):
    pairs = [(line(x, y, z, core), line(x, y, z, 1 - core)) for x, y, z, core in CHIPS]
    return lax.ppermute(array, BOTH, pairs)


def row_order():
    place = jnp.arange(C, dtype=jnp.int32)
    far, x, y, z, row = place // 512, place // 128 % 4, place // 32 % 4, place // 4 % 8, place % 4
    core = (lax.axis_index("row") + far) % 2
    source = z * 128 + x // 2 * 64 + core * 32 + y * 8 + x % 2 * 4 + row
    return (source[:, None] == jnp.arange(C, dtype=jnp.int32)[None, :]).astype(BF)


def plus(*terms):
    return sum(term.astype(F32) for term in terms).astype(BF)


def group_sum(blocks, groups):
    got = lax.all_to_all(blocks, BOTH, 0, 0, axis_index_groups=groups, tiled=True)
    return jnp.sum(got.astype(F32), axis=0)


def plane_sum(blocks):
    groups = [
        [line(x, y, z, core) for x in range(4) for y in range(4)]
        for z in range(8)
        for core in range(2)
    ]
    return group_sum(blocks, groups).astype(BF)


def z_sum(blocks):
    groups = [
        [line(x, y, z, core) for z in range(8)]
        for x in range(4)
        for y in range(4)
        for core in range(2)
    ]
    return group_sum(blocks, groups)


def per_device(tokens, grad_out, w_qkv, w_proj, norm_gain, logit_scale):
    rows, cols = lax.axis_size("row"), lax.axis_size("col")
    x = window(tokens, rows, cols)
    g = window(grad_out, rows, cols)
    att, probs, query, key, value, unit_scale = attention(x, w_qkv, logit_scale, rows, cols)
    order = row_order()
    proj, far, grad_att = output_norm(att, g, order, w_proj, norm_gain.reshape(1, C))
    proj_far = other_core(far)
    val, far, grad_value = value_grads(x, order, probs, grad_att)
    terms = jnp.concatenate(
        [
            plus(proj, proj_far).reshape(16, 32, C),
            plus(val, other_core(far)).reshape(16, 32, C),
        ],
        axis=1,
    )

    grad_query, grad_key = score_grads(
        probs, grad_att, query, key, value, unit_scale, logit_scale, terms
    )
    terms = plane_sum(terms)
    grad_input = input_grad([grad_query, grad_key, grad_value], w_qkv)
    terms = jnp.concatenate(
        [terms[:32].reshape(8, 4, C), terms[32:].reshape(8, 4, C)], axis=1
    )
    terms = z_sum(terms)
    proj_part, value_part = terms[:4], terms[4:]
    back = jnp.stack(
        [
            passed(grad_input[3], 1, 1, rows, cols),
            passed(grad_input[2], 1, 0, rows, cols),
            passed(grad_input[1], 0, 1, rows, cols),
            grad_input[0],
        ]
    )
    back = back.reshape(2, 2, HALF, HALF, C).transpose(0, 2, 1, 3, 4).reshape(WIN, WIN, C)
    grad_tokens = (grad_out.astype(F32) + back.astype(F32)).astype(BF)
    return (grad_tokens, value_part, proj_part)


def solution(mesh):
    in_specs = (P("row", "col", None), P("row", "col", None), P(), P(), P(), P())
    out_specs = (P("row", "col", None), P(("row", "col"), None), P(("row", "col"), None))
    return jax.shard_map(
        per_device, mesh=mesh, in_specs=in_specs, out_specs=out_specs, check_vma=False
    )
```

```python
import functools
import math

import jax
import jax.numpy as jnp
from jax import lax
from jax.experimental import pallas as pl
from jax.experimental.pallas import tpu as pltpu
from jax.sharding import PartitionSpec as P

HEADS = 32
WIN = 16
HALF = WIN // 2
DIM = 32
TOK = WIN * WIN
C = 1024
EPS_NORM = 1e-06
EPS_LN = 1e-05
LOG2E = math.log2(math.e)
BLOCK = 2.0**20
BF = jnp.bfloat16
F32 = jnp.float32
MIB = 2**20


def dot(left, right, dims=((1,), (0,))):
    return lax.dot_general(left, right, (dims, ((), ())), preferred_element_type=F32)


TN = ((0,), (0,))
NT = ((1,), (1,))
TT = ((0,), (1,))


def head_rows(h):
    return pl.ds(pl.multiple_of(h * DIM, DIM), DIM)


def last_window(rows, cols):
    last_row = (lax.axis_index("row") == rows - 1).astype(F32)
    last_col = (lax.axis_index("col") == cols - 1).astype(F32)
    return last_row, last_col


def mask_features(last_row, last_col):
    feature = lax.broadcasted_iota(jnp.int32, (16, TOK), 0)
    token = lax.broadcasted_iota(jnp.int32, (16, TOK), 1)
    low = (token // (TOK // 2)).astype(F32)
    far = (token // (TOK // 4) % 2).astype(F32)

    def rows(*values):
        out = jnp.zeros((16, TOK), F32)
        for n, value in enumerate(values):
            out = jnp.where(feature == n, value, out)
        return out

    key = rows(low, 1 - low, far, 1 - far)
    query = -BLOCK * rows(
        last_row * (1 - low), last_row * low, last_col * (1 - far), last_col * far
    )
    return key.astype(BF), query.astype(BF)


def attention_kernel(
    rows, cols, x0_ref, x1_ref, x2_ref, x3_ref, w_hbm_ref, scale_ref,
    att_ref, probs_ref, query_ref, key_ref, value_ref, unit_scale_ref, window_ref,
    w_qkv_ref, sems,
):
    copies = []
    for n in range(3):
        span = pl.ds(n * C, C)
        copies.append(
            pltpu.make_async_copy(w_hbm_ref.at[:, span], w_qkv_ref.at[:, span], sems.at[n])
        )
        copies[-1].start()
    key_mask, query_mask = mask_features(*last_window(rows, cols))
    x = jnp.concatenate([x0_ref[...], x1_ref[...], x2_ref[...], x3_ref[...]], axis=0)
    window_ref[...] = x
    for col in range(0, 3 * C, TOK):
        if col % C == 0:
            copies[col // C].wait()
        raw = dot(x, w_qkv_ref[:, col : col + TOK]).T
        if col < 2 * C:
            heads = raw.reshape(TOK // DIM, DIM, TOK)
            inv = lax.rsqrt(jnp.sum(heads * heads, axis=1, keepdims=True) + EPS_NORM)
            unit = (heads * inv).reshape(TOK, TOK)
            unit_scale_ref[col // DIM : (col + TOK) // DIM, :] = inv[:, 0, :]
            if col < C:
                query_ref[col : col + TOK, :] = unit
            else:
                key_ref[col - C : col - C + TOK, :] = unit
        else:
            value_ref[col - 2 * C : col - 2 * C + TOK, :] = raw.astype(BF)

    def head(h, carry):
        rows = head_rows(h)
        raw = dot(
            jnp.concatenate([key_ref[rows, :].astype(BF), key_mask], axis=0),
            jnp.concatenate([query_ref[rows, :].astype(BF), query_mask], axis=0),
            TN,
        )
        top = jnp.max(raw, axis=0, keepdims=True)
        expo = jnp.exp2((raw - top) * (scale_ref[h] * LOG2E))
        probs = expo * (1.0 / jnp.sum(expo, axis=0, keepdims=True))
        probs_ref[h] = probs
        att_ref[rows, :] = dot(probs.astype(BF), value_ref[rows, :], TT).T.astype(BF)
        return carry

    lax.fori_loop(0, HEADS, head, 0, unroll=8)


def norm_kernel(
    att_ref, g0_ref, g1_ref, g2_ref, g3_ref, w_proj_ref, gain_ref, grad_mix_ref, grad_att_ref
):
    g = jnp.concatenate([g0_ref[...], g1_ref[...], g2_ref[...], g3_ref[...]], axis=0)
    mixed = dot(att_ref[...], w_proj_ref[...], TN)
    center = mixed - jnp.mean(mixed, axis=-1, keepdims=True)
    inv_std = lax.rsqrt(jnp.mean(center * center, axis=-1, keepdims=True) + EPS_LN)
    normed = center * inv_std
    grad_norm = g.astype(F32) * gain_ref[...]
    grad_mix = inv_std * (
        grad_norm
        - jnp.mean(grad_norm, axis=-1, keepdims=True)
        - normed * jnp.mean(grad_norm * normed, axis=-1, keepdims=True)
    )
    grad_mix = grad_mix.astype(BF)
    grad_mix_ref[...] = grad_mix
    for row in range(0, C, TOK):
        grad_att_ref[row : row + TOK, :] = dot(
            w_proj_ref[row : row + TOK, :], grad_mix, NT
        ).astype(BF)


def value_kernel(probs_ref, grad_att_ref, grad_value_ref):
    def head(h, carry):
        rows = head_rows(h)
        grad_value_ref[rows, :] = dot(
            grad_att_ref[rows, :], probs_ref[h].astype(BF), NT
        ).astype(BF)
        return carry

    lax.fori_loop(0, HEADS, head, 0, unroll=8)


def write_blocks(out_refs, col, term):
    for n, out_ref in enumerate(out_refs):
        out_ref[:, col : col + TOK] = term[n * 128 : n * 128 + 128].astype(BF)


def proj_term_kernel(order_ref, att_ref, att2_ref, grad_mix_ref, grad_mix2_ref, *out_refs):
    att = jnp.concatenate([att_ref[...], att2_ref[...]], axis=1)
    grad_mix = jnp.concatenate([grad_mix_ref[...], grad_mix2_ref[...]], axis=0)
    left = dot(order_ref[...], att).astype(BF)
    for col in range(0, C, TOK):
        write_blocks(out_refs, col, dot(left, grad_mix[:, col : col + TOK]))


def value_term_kernel(order_ref, x_ref, x2_ref, grad_value_ref, grad_value2_ref, *out_refs):
    x = jnp.concatenate([x_ref[...], x2_ref[...]], axis=0)
    grad_value = jnp.concatenate([grad_value_ref[...], grad_value2_ref[...]], axis=1)
    left = dot(order_ref[...], x, NT).astype(BF)
    for col in range(0, C, TOK):
        write_blocks(out_refs, col, dot(left, grad_value[col : col + TOK, :], NT))


def sum_kernel(*refs):
    ins, out_refs = refs[:8], refs[8:]
    for group in range(2):
        own, *others = ins[group * 4 : group * 4 + 4]
        total = own[...].astype(F32)
        for other in others:
            total += other[...].astype(F32)
        total = total.astype(BF)
        for n in range(4):
            out_refs[group * 4 + n][...] = total[n * 32 : n * 32 + 32]


def score_kernel(
    first, count, probs_ref, grad_att_ref, query_ref, key_ref, value_ref, unit_scale_ref,
    scale_ref, after_ref, grad_query_ref, grad_key_ref, grad_score_ref,
):
    def scores(n, carry):
        h = n + first
        rows = head_rows(h)
        probs = probs_ref[h]
        grad_prob = dot(value_ref[rows, :], grad_att_ref[rows, :], TN)
        mean = jnp.sum(grad_prob * probs, axis=0, keepdims=True)
        grad_score_ref[n] = (scale_ref[h] * (probs * (grad_prob - mean))).astype(BF)
        return carry

    def units(n, carry):
        h = n + first
        rows, out_rows = head_rows(h), head_rows(n)
        query = query_ref[rows, :]
        key = key_ref[rows, :]
        grad_score = grad_score_ref[n]
        grad_query = dot(key.astype(BF), grad_score)
        grad_key = dot(grad_score, query.astype(BF), NT).T
        grad_query = unit_scale_ref[pl.ds(h, 1), :] * (
            grad_query - query * jnp.sum(grad_query * query, axis=0, keepdims=True)
        )
        grad_key = unit_scale_ref[pl.ds(h + HEADS, 1), :] * (
            grad_key - key * jnp.sum(grad_key * key, axis=0, keepdims=True)
        )
        grad_query_ref[out_rows, :] = grad_query.astype(BF)
        grad_key_ref[out_rows, :] = grad_key.astype(BF)
        return carry

    lax.fori_loop(0, count, scores, 0, unroll=8)
    lax.fori_loop(0, count, units, 0, unroll=16)


def input_kernel(*refs):
    parts, w_qkv_ref, out_refs = refs[:-5], refs[-5], refs[-4:]
    for row in range(0, C, TOK):
        total, col = 0.0, 0
        for part in parts:
            size = part.shape[0]
            total += dot(w_qkv_ref[row : row + TOK, col : col + size], part[...])
            col += size
        total = total.T.astype(BF)
        for n, out_ref in enumerate(out_refs):
            out_ref[:, row : row + TOK] = total[n * 64 : n * 64 + 64]


VM = pl.BlockSpec(memory_space=pltpu.VMEM)
SM = pl.BlockSpec(memory_space=pltpu.SMEM)


def shape(dims, kind):
    return jax.ShapeDtypeStruct(dims, kind)


def call(kernel, outs, ins, micros, name, limit, scratch=()):
    return pl.pallas_call(
        kernel,
        out_shape=outs,
        in_specs=ins,
        out_specs=jax.tree.map(lambda _: VM, outs),
        scratch_shapes=scratch,
        compiler_params=pltpu.CompilerParams(vmem_limit_bytes=limit * MIB),
        cost_estimate=pl.CostEstimate(
            flops=int(micros * 11 * 10**8), bytes_accessed=MIB, transcendentals=0
        ),
        name=name,
    )


def attention(quads, w_qkv, scale, rows, cols):
    flat = shape((C, TOK), F32)
    flat_bf = shape((C, TOK), BF)
    outs = (
        flat_bf, shape((HEADS, TOK, TOK), F32), flat, flat, flat_bf, shape((2 * HEADS, TOK), F32),
        shape((TOK, C), BF),
    )
    kernel = functools.partial(attention_kernel, rows, cols)
    scratch = [pltpu.VMEM((C, 3 * C), BF), pltpu.SemaphoreType.DMA((3,))]
    return call(
        kernel, outs, [VM] * 4 + [pl.BlockSpec(memory_space=pltpu.HBM), SM], 14,
        "attention_part", 24, scratch,
    )(*quads, pltpu.with_memory_space_constraint(w_qkv, pltpu.HBM), scale)


def output_norm(att, quads, w_proj, gain):
    outs = (shape((TOK, C), BF), shape((C, TOK), BF))
    return call(norm_kernel, outs, [VM] * 7, 2, "norm_part", 24)(att, *quads, w_proj, gain)


def value_grads(probs, grad_att):
    return call(value_kernel, shape((C, TOK), BF), [VM] * 2, 2, "value_part", 24)(probs, grad_att)


def proj_terms(*args):
    return call(proj_term_kernel, (shape((128, C), BF),) * 4, [VM] * 5, 1.3, "proj_term", 24)(*args)


def value_terms(*args):
    return call(value_term_kernel, (shape((128, C), BF),) * 4, [VM] * 5, 1.3, "value_term", 24)(*args)


def score_grads(first, count, *args):
    outs = (shape((count * DIM, TOK), BF),) * 2
    scratch = [pltpu.VMEM((count, TOK, TOK), BF)]
    kernel = functools.partial(score_kernel, first, count)
    ins = [VM] * 6 + [SM, pl.BlockSpec(memory_space=pl.ANY)]
    return call(kernel, outs, ins, 0.3, "score_part", 32, scratch)(*args)


def block_sums(blocks):
    return call(sum_kernel, (shape((32, C), BF),) * 8, [VM] * 8, 0.5, "block_sums", 24)(*blocks)


def input_grad(parts, w_qkv):
    outs = (shape((TOK // 4, C), BF),) * 4
    return call(input_kernel, outs, [VM] * (len(parts) + 1), 0.2, "input_part", 24)(*parts, w_qkv)


def passed(array, d_row, d_col, rows, cols):
    pairs = [
        (r * cols + c, (r + d_row) % rows * cols + (c + d_col) % cols)
        for r in range(rows)
        for c in range(cols)
    ]
    return lax.ppermute(array, ("row", "col"), pairs)


def window(array, rows, cols):
    def quad(r, c):
        return array[r : r + HALF, c : c + HALF].reshape(TOK // 4, C)

    return (
        quad(HALF, HALF),
        passed(quad(HALF, 0), 0, -1, rows, cols),
        passed(quad(0, HALF), -1, 0, rows, cols),
        passed(quad(0, 0), -1, -1, rows, cols),
    )


def line(x, y, z, core):
    return ((z * 2 + x // 2) * 2 + core) * 8 + y * 2 + x % 2


CHIPS = [(x, y, z, core) for x in range(4) for y in range(4) for z in range(8) for core in range(2)]
BOTH = ("row", "col")


def other_core(array):
    pairs = [(line(x, y, z, core), line(x, y, z, 1 - core)) for x, y, z, core in CHIPS]
    return lax.ppermute(array, BOTH, pairs)


def moved(array, axis, by):
    pairs = []
    for x, y, z, core in CHIPS:
        to = ((x + by) % 4, y) if axis == "x" else (x, (y + by) % 4)
        pairs.append((line(x, y, z, core), line(*to, z, core)))
    return lax.ppermute(array, BOTH, pairs)


def gathered(blocks, axis):
    far = moved(blocks[2], axis, 2)
    return far, moved(blocks[1], axis, 1), moved(blocks[3], axis, -1)


def row_order(axis):
    place = jnp.arange(C // 2, dtype=jnp.int32)
    a, b, z, row = place // 128, place // 32 % 4, place // 4 % 8, place % 4
    r, c = lax.axis_index("row"), lax.axis_index("col")
    dx, dy = (a, b) if axis == "x" else (b, a)
    x = (r // 2 % 2 * 2 + c % 2 + dx) % 4
    y = (c // 2 + dy) % 4
    source = z * 128 + x // 2 * 64 + r % 2 * 32 + y * 8 + x % 2 * 4 + row
    return (source[:, None] == jnp.arange(C, dtype=jnp.int32)[None, :]).astype(BF)


def group_sum(blocks, groups):
    got = lax.all_to_all(blocks, BOTH, 0, 0, axis_index_groups=groups, tiled=True)
    return jnp.sum(got.astype(F32), axis=0)


def z_sum(blocks):
    groups = [
        [line(x, y, z, core) for z in range(8)]
        for x in range(4)
        for y in range(4)
        for core in range(2)
    ]
    return group_sum(blocks, groups)


def per_device(tokens, grad_out, w_qkv, w_proj, norm_gain, logit_scale):
    rows, cols = lax.axis_size("row"), lax.axis_size("col")
    x = window(tokens, rows, cols)
    g = window(grad_out, rows, cols)
    att, probs, query, key, value, unit_scale, tokens_win = attention(
        x, w_qkv, logit_scale, rows, cols
    )
    grad_mix, grad_att = output_norm(att, g, w_proj, norm_gain.reshape(1, C))
    grad_value = value_grads(probs, grad_att)
    proj = proj_terms(row_order("x"), att, other_core(att), grad_mix, other_core(grad_mix))
    val = value_terms(
        row_order("y"), tokens_win, other_core(tokens_win), grad_value, other_core(grad_value)
    )
    proj_got, val_got = gathered(proj, "x"), gathered(val, "y")
    args = (probs, grad_att, query, key, value, unit_scale, logit_scale)
    half = HEADS // 2
    early = score_grads(0, half, *args, val[0])
    late = score_grads(half, half, *args, proj_got[0])
    parts = [early[0], late[0], early[1], late[1], grad_value]
    grad_input = input_grad(parts, w_qkv)
    grad_input, proj_got, val_got = lax.optimization_barrier((grad_input, proj_got, val_got))
    blocks = block_sums((proj[0], *proj_got, val[0], *val_got))
    proj, val = blocks[:4], blocks[4:]
    proj_got, val_got = gathered(proj, "y"), gathered(val, "x")
    proj, val, grad_input = lax.optimization_barrier(
        ((proj[0], *proj_got), (val[0], *val_got), grad_input)
    )
    terms = jnp.concatenate(
        [sum(a.astype(F32) for a in part).reshape(8, 4, C).astype(BF) for part in (proj, val)],
        axis=1,
    )
    terms = z_sum(terms)
    proj_part, value_part = terms[:4], terms[4:]
    back = jnp.stack(
        [
            passed(grad_input[3], 1, 1, rows, cols),
            passed(grad_input[2], 1, 0, rows, cols),
            passed(grad_input[1], 0, 1, rows, cols),
            grad_input[0],
        ]
    )
    back = back.reshape(2, 2, HALF, HALF, C).transpose(0, 2, 1, 3, 4).reshape(WIN, WIN, C)
    grad_tokens = (grad_out.astype(F32) + back.astype(F32)).astype(BF)
    return (grad_tokens, value_part, proj_part)


def solution(mesh):
    in_specs = (P("row", "col", None), P("row", "col", None), P(), P(), P(), P())
    out_specs = (P("row", "col", None), P(("row", "col"), None), P(("row", "col"), None))
    return jax.shard_map(
        per_device, mesh=mesh, in_specs=in_specs, out_specs=out_specs, check_vma=False
    )
```

```python
import functools
import math

import jax
import jax.numpy as jnp
from jax import lax
from jax.experimental import pallas as pl
from jax.experimental.pallas import tpu as pltpu
from jax.sharding import PartitionSpec as P

HEADS = 32
WIN = 16
HALF = WIN // 2
DIM = 32
TOK = WIN * WIN
C = 1024
EPS_NORM = 1e-06
EPS_LN = 1e-05
LOG2E = math.log2(math.e)
BLOCK = 2.0**20
BF = jnp.bfloat16
F32 = jnp.float32
MIB = 2**20


def dot(left, right, dims=((1,), (0,))):
    return lax.dot_general(left, right, (dims, ((), ())), preferred_element_type=F32)


TN = ((0,), (0,))
NT = ((1,), (1,))
TT = ((0,), (1,))
EARLY = 8


def head_rows(h):
    return pl.ds(pl.multiple_of(h * DIM, DIM), DIM)


def core_index():
    return lax.rem(lax.axis_index("row"), 2)


def last_window(rows, cols):
    last_row = (lax.axis_index("row") == rows - 1).astype(F32)
    last_col = (lax.axis_index("col") == cols - 1).astype(F32)
    return last_row, last_col


def mask_features(last_row, last_col):
    feature = lax.broadcasted_iota(jnp.int32, (16, TOK), 0)
    token = lax.broadcasted_iota(jnp.int32, (16, TOK), 1)
    low = (token // (TOK // 2)).astype(F32)
    far = (token // (TOK // 4) % 2).astype(F32)

    def rows(*values):
        out = jnp.zeros((16, TOK), F32)
        for n, value in enumerate(values):
            out = jnp.where(feature == n, value, out)
        return out

    key = rows(low, 1 - low, far, 1 - far)
    query = -BLOCK * rows(
        last_row * (1 - low), last_row * low, last_col * (1 - far), last_col * far
    )
    return key.astype(BF), query.astype(BF)


def attention_kernel(
    rows, cols, x0_ref, x1_ref, x2_ref, x3_ref, w_hbm_ref, scale_ref, after_ref,
    att_ref, probs_ref, query_ref, key_ref, value_ref, unit_scale_ref, window_ref,
    w_qkv_ref, sems,
):
    copies = []
    for n in range(3):
        span = pl.ds(n * C, C)
        copies.append(
            pltpu.make_async_copy(w_hbm_ref.at[:, span], w_qkv_ref.at[:, span], sems.at[n])
        )
        copies[-1].start()
    key_mask, query_mask = mask_features(*last_window(rows, cols))
    x = jnp.concatenate([x0_ref[...], x1_ref[...], x2_ref[...], x3_ref[...]], axis=0)
    window_ref[...] = x
    for col in range(0, 3 * C, TOK):
        if col % C == 0:
            copies[col // C].wait()
        raw = dot(x, w_qkv_ref[:, col : col + TOK]).T
        if col < 2 * C:
            heads = raw.reshape(TOK // DIM, DIM, TOK)
            inv = lax.rsqrt(jnp.sum(heads * heads, axis=1, keepdims=True) + EPS_NORM)
            unit = (heads * inv).reshape(TOK, TOK)
            unit_scale_ref[col // DIM : (col + TOK) // DIM, :] = inv[:, 0, :]
            if col < C:
                query_ref[col : col + TOK, :] = unit
            else:
                key_ref[col - C : col - C + TOK, :] = unit
        else:
            value_ref[col - 2 * C : col - 2 * C + TOK, :] = raw.astype(BF)

    def head(h, carry):
        rows = head_rows(h)
        raw = dot(
            jnp.concatenate([key_ref[rows, :].astype(BF), key_mask], axis=0),
            jnp.concatenate([query_ref[rows, :].astype(BF), query_mask], axis=0),
            TN,
        )
        top = jnp.max(raw, axis=0, keepdims=True)
        expo = jnp.exp2((raw - top) * (scale_ref[h] * LOG2E))
        probs = expo * (1.0 / jnp.sum(expo, axis=0, keepdims=True))
        probs_ref[h] = probs
        att_ref[rows, :] = dot(probs.astype(BF), value_ref[rows, :], TT).T.astype(BF)
        return carry

    lax.fori_loop(0, HEADS, head, 0, unroll=8)


def norm_kernel(
    att_ref, g0_ref, g1_ref, g2_ref, g3_ref, w_proj_ref, gain_ref, grad_mix_ref, grad_att_ref
):
    g = jnp.concatenate([g0_ref[...], g1_ref[...], g2_ref[...], g3_ref[...]], axis=0)
    mixed = dot(att_ref[...], w_proj_ref[...], TN)
    center = mixed - jnp.mean(mixed, axis=-1, keepdims=True)
    inv_std = lax.rsqrt(jnp.mean(center * center, axis=-1, keepdims=True) + EPS_LN)
    normed = center * inv_std
    grad_norm = g.astype(F32) * gain_ref[...]
    grad_mix = inv_std * (
        grad_norm
        - jnp.mean(grad_norm, axis=-1, keepdims=True)
        - normed * jnp.mean(grad_norm * normed, axis=-1, keepdims=True)
    )
    grad_mix = grad_mix.astype(BF)
    grad_mix_ref[...] = grad_mix
    for row in range(0, C, TOK):
        grad_att_ref[row : row + TOK, :] = dot(
            w_proj_ref[row : row + TOK, :], grad_mix, NT
        ).astype(BF)


def value_kernel(probs_ref, grad_att_ref, grad_value_ref):
    def head(h, carry):
        rows = head_rows(h)
        grad_value_ref[rows, :] = dot(
            grad_att_ref[rows, :], probs_ref[h].astype(BF), NT
        ).astype(BF)
        return carry

    lax.fori_loop(0, HEADS, head, 0, unroll=8)


def term_kernel(
    order_ref, att_ref, x_ref, grad_mix_ref, grad_value_ref,
    att2_ref, x2_ref, grad_mix2_ref, grad_value2_ref, after_ref, *out_refs,
):
    def write(col, term):
        for n, out_ref in enumerate(out_refs):
            out_ref[:, col : col + TOK] = term[n * TOK : n * TOK + TOK].astype(BF)

    @pl.when(core_index() == 0)
    def _():
        att = jnp.concatenate([att_ref[...], att2_ref[...]], axis=1)
        grad_mix = jnp.concatenate([grad_mix_ref[...], grad_mix2_ref[...]], axis=0)
        left = dot(order_ref[...], att).astype(BF)
        for col in range(0, C, TOK):
            write(col, dot(left, grad_mix[:, col : col + TOK]))

    @pl.when(core_index() == 1)
    def _():
        x = jnp.concatenate([x_ref[...], x2_ref[...]], axis=0)
        grad_value = jnp.concatenate([grad_value_ref[...], grad_value2_ref[...]], axis=1)
        left = dot(order_ref[...], x, NT).astype(BF)
        for col in range(0, C, TOK):
            write(col, dot(left, grad_value[col : col + TOK, :], NT))


def sum_kernel(own_ref, *refs):
    total = own_ref[...].astype(F32)
    for other in refs[:3]:
        total += other[...].astype(F32)
    total = total.astype(BF)
    size = total.shape[0] // len(refs[3:])
    for n, out_ref in enumerate(refs[3:]):
        out_ref[...] = total[n * size : n * size + size]


def score_kernel(
    first, count, probs_ref, grad_att_ref, query_ref, key_ref, value_ref, unit_scale_ref,
    scale_ref, after_ref, grad_query_ref, grad_key_ref, grad_score_ref,
):
    def scores(n, carry):
        h = n + first
        rows = head_rows(h)
        probs = probs_ref[h]
        grad_prob = dot(value_ref[rows, :], grad_att_ref[rows, :], TN)
        mean = jnp.sum(grad_prob * probs, axis=0, keepdims=True)
        grad_score_ref[n] = (scale_ref[h] * (probs * (grad_prob - mean))).astype(BF)
        return carry

    def units(n, carry):
        h = n + first
        rows, out_rows = head_rows(h), head_rows(n)
        query = query_ref[rows, :]
        key = key_ref[rows, :]
        grad_score = grad_score_ref[n]
        grad_query = dot(key.astype(BF), grad_score)
        grad_key = dot(grad_score, query.astype(BF), NT).T
        grad_query = unit_scale_ref[pl.ds(h, 1), :] * (
            grad_query - query * jnp.sum(grad_query * query, axis=0, keepdims=True)
        )
        grad_key = unit_scale_ref[pl.ds(h + HEADS, 1), :] * (
            grad_key - key * jnp.sum(grad_key * key, axis=0, keepdims=True)
        )
        grad_query_ref[out_rows, :] = grad_query.astype(BF)
        grad_key_ref[out_rows, :] = grad_key.astype(BF)
        return carry

    lax.fori_loop(0, count, scores, 0, unroll=8)
    lax.fori_loop(0, count, units, 0, unroll=8)


def input_kernel(*refs):
    parts, w_qkv_ref, out_refs = refs[:-5], refs[-5], refs[-4:]
    for row in range(0, C, TOK):
        total, col = 0.0, 0
        for part in parts:
            size = part.shape[0]
            total += dot(w_qkv_ref[row : row + TOK, col : col + size], part[...])
            col += size
        total = total.T.astype(BF)
        for n, out_ref in enumerate(out_refs):
            out_ref[:, row : row + TOK] = total[n * 64 : n * 64 + 64]


VM = pl.BlockSpec(memory_space=pltpu.VMEM)
SM = pl.BlockSpec(memory_space=pltpu.SMEM)


def shape(dims, kind):
    return jax.ShapeDtypeStruct(dims, kind)


def call(kernel, outs, ins, micros, name, limit, scratch=()):
    return pl.pallas_call(
        kernel,
        out_shape=outs,
        in_specs=ins,
        out_specs=jax.tree.map(lambda _: VM, outs),
        scratch_shapes=scratch,
        compiler_params=pltpu.CompilerParams(vmem_limit_bytes=limit * MIB),
        cost_estimate=pl.CostEstimate(
            flops=int(micros * 11 * 10**8), bytes_accessed=MIB, transcendentals=0
        ),
        name=name,
    )


def attention(quads, w_qkv, scale, rows, cols, after):
    flat = shape((C, TOK), F32)
    flat_bf = shape((C, TOK), BF)
    outs = (
        flat_bf, shape((HEADS, TOK, TOK), F32), flat, flat, flat_bf, shape((2 * HEADS, TOK), F32),
        shape((TOK, C), BF),
    )
    kernel = functools.partial(attention_kernel, rows, cols)
    scratch = [pltpu.VMEM((C, 3 * C), BF), pltpu.SemaphoreType.DMA((3,))]
    return call(
        kernel, outs, [VM] * 4 + [pl.BlockSpec(memory_space=pltpu.HBM), SM, pl.BlockSpec(memory_space=pl.ANY)], 14,
        "attention_part", 24, scratch,
    )(*quads, pltpu.with_memory_space_constraint(w_qkv, pltpu.HBM), scale, after)


def output_norm(att, quads, w_proj, gain):
    outs = (shape((TOK, C), BF), shape((C, TOK), BF))
    return call(norm_kernel, outs, [VM] * 7, 2, "norm_part", 16)(att, *quads, w_proj, gain)


def value_grads(probs, grad_att):
    return call(value_kernel, shape((C, TOK), BF), [VM] * 2, 2, "value_part", 16)(probs, grad_att)


def weight_terms(*args):
    ins = [VM] * 9 + [pl.BlockSpec(memory_space=pl.ANY)]
    return call(term_kernel, (shape((TOK, C), BF),) * 4, ins, 2.6, "weight_terms", 24)(*args)


def score_grads(first, count, *args):
    outs = (shape((count * DIM, TOK), BF),) * 2
    scratch = [pltpu.VMEM((count, TOK, TOK), BF)]
    kernel = functools.partial(score_kernel, first, count)
    ins = [VM] * 6 + [SM, pl.BlockSpec(memory_space=pl.ANY)]
    return call(kernel, outs, ins, 0.3, "score_part", 16, scratch)(*args)


def block_sums(count, *blocks):
    outs = (shape((64, C), BF),) * count
    return call(sum_kernel, outs, [VM] * 4, 0.5, "block_sums", 16)(*blocks)


def input_grad(parts, w_qkv):
    outs = (shape((TOK // 4, C), BF),) * 4
    return call(input_kernel, outs, [VM] * (len(parts) + 1), 0.2, "input_part", 24)(*parts, w_qkv)


def passed(array, d_row, d_col, rows, cols):
    pairs = [
        (r * cols + c, (r + d_row) % rows * cols + (c + d_col) % cols)
        for r in range(rows)
        for c in range(cols)
    ]
    return lax.ppermute(array, ("row", "col"), pairs)


def window(array, rows, cols):
    def quad(r, c):
        return array[r : r + HALF, c : c + HALF].reshape(TOK // 4, C)

    return (
        quad(HALF, HALF),
        passed(quad(HALF, 0), 0, -1, rows, cols),
        passed(quad(0, HALF), -1, 0, rows, cols),
        passed(quad(0, 0), -1, -1, rows, cols),
    )


def line(x, y, z, core):
    return ((z * 2 + x // 2) * 2 + core) * 8 + y * 2 + x % 2


CHIPS = [(x, y, z, core) for x in range(4) for y in range(4) for z in range(8) for core in range(2)]
BOTH = ("row", "col")


def other_core(array):
    pairs = [(line(x, y, z, core), line(x, y, z, 1 - core)) for x, y, z, core in CHIPS]
    return lax.ppermute(array, BOTH, pairs)


def moved(array, stage, by):
    pairs = []
    for x, y, z, core in CHIPS:
        to = ((x + by) % 4, y) if core == stage else (x, (y + by) % 4)
        pairs.append((line(x, y, z, core), line(*to, z, core)))
    return lax.ppermute(array, BOTH, pairs)


def gathered(blocks, stage):
    far = moved(blocks[2], stage, 2)
    return far, moved(blocks[1], stage, 1), moved(blocks[3], stage, -1)


def row_order():
    place = jnp.arange(C, dtype=jnp.int32)
    a, b, z, far, row = place // 256, place // 64 % 4, place // 8 % 8, place // 4 % 2, place % 4
    r, c = lax.axis_index("row"), lax.axis_index("col")
    core = r % 2
    dx, dy = jnp.where(core == 0, a, b), jnp.where(core == 0, b, a)
    x = (r // 2 % 2 * 2 + c % 2 + dx) % 4
    y = (c // 2 + dy) % 4
    source = z * 128 + x // 2 * 64 + (core + far) % 2 * 32 + y * 8 + x % 2 * 4 + row
    return (source[:, None] == jnp.arange(C, dtype=jnp.int32)[None, :]).astype(BF)


def group_sum(blocks, groups):
    got = lax.all_to_all(blocks, BOTH, 0, 0, axis_index_groups=groups, tiled=True)
    return jnp.sum(got.astype(F32), axis=0)


def z_sum(blocks):
    groups = [
        [line(x, y, z, core) for z in range(8)]
        for x in range(4)
        for y in range(4)
        for core in range(2)
    ]
    return group_sum(blocks, groups)


def per_device(tokens, grad_out, w_qkv, w_proj, norm_gain, logit_scale):
    rows, cols = lax.axis_size("row"), lax.axis_size("col")
    x = window(tokens, rows, cols)
    g = window(grad_out, rows, cols)
    order = row_order()
    att, probs, query, key, value, unit_scale, tokens_win = attention(
        x, w_qkv, logit_scale, rows, cols, order
    )
    grad_mix, grad_att = output_norm(att, g, w_proj, norm_gain.reshape(1, C))
    grad_value = value_grads(probs, grad_att)
    mine = (att, tokens_win, grad_mix, grad_value)
    args = (probs, grad_att, query, key, value, unit_scale, logit_scale)
    early = score_grads(0, EARLY, *args, grad_value)
    blocks = weight_terms(order, *mine, *[other_core(a) for a in mine], early[0])
    others = gathered(blocks, 0)
    late = score_grads(EARLY, HEADS - EARLY, *args, blocks[0])
    parts = [early[0], late[0], early[1], late[1], grad_value]
    grad_input = input_grad(parts, w_qkv)
    grad_input, others = lax.optimization_barrier((grad_input, others))
    blocks = block_sums(4, blocks[0], *others)
    others = gathered(blocks, 1)
    terms, grad_input = lax.optimization_barrier(((blocks[0], *others), grad_input))
    (terms,) = block_sums(1, *terms)
    terms = z_sum(terms.reshape(8, 8, C))
    kept, got = terms[:4], other_core(terms[4:])
    first = lax.axis_index("row") % 2 == 0
    proj_part, value_part = jnp.where(first, kept, got), jnp.where(first, got, kept)
    back = jnp.stack(
        [
            passed(grad_input[3], 1, 1, rows, cols),
            passed(grad_input[2], 1, 0, rows, cols),
            passed(grad_input[1], 0, 1, rows, cols),
            grad_input[0],
        ]
    )
    back = back.reshape(2, 2, HALF, HALF, C).transpose(0, 2, 1, 3, 4).reshape(WIN, WIN, C)
    grad_tokens = (grad_out.astype(F32) + back.astype(F32)).astype(BF)
    return (grad_tokens, value_part, proj_part)


def solution(mesh):
    in_specs = (P("row", "col", None), P("row", "col", None), P(), P(), P(), P())
    out_specs = (P("row", "col", None), P(("row", "col"), None), P(("row", "col"), None))
    return jax.shard_map(
        per_device, mesh=mesh, in_specs=in_specs, out_specs=out_specs, check_vma=False
    )
```

```python
import functools
import math

import jax
import jax.numpy as jnp
from jax import lax
from jax.experimental import pallas as pl
from jax.experimental.pallas import tpu as pltpu
from jax.sharding import PartitionSpec as P

HEADS = 32
WIN = 16
HALF = WIN // 2
DIM = 32
TOK = WIN * WIN
C = 1024
EPS_NORM = 1e-06
EPS_LN = 1e-05
LOG2E = math.log2(math.e)
BLOCK = 2.0**20
BF = jnp.bfloat16
F32 = jnp.float32
MIB = 2**20


def dot(left, right, dims=((1,), (0,))):
    return lax.dot_general(left, right, (dims, ((), ())), preferred_element_type=F32)


TN = ((0,), (0,))
NT = ((1,), (1,))
TT = ((0,), (1,))


def head_rows(h):
    return pl.ds(pl.multiple_of(h * DIM, DIM), DIM)


def core_index():
    return lax.rem(lax.axis_index("row"), 2)


def last_window(rows, cols):
    last_row = (lax.axis_index("row") == rows - 1).astype(F32)
    last_col = (lax.axis_index("col") == cols - 1).astype(F32)
    return last_row, last_col


def mask_features(last_row, last_col):
    feature = lax.broadcasted_iota(jnp.int32, (16, TOK), 0)
    token = lax.broadcasted_iota(jnp.int32, (16, TOK), 1)
    low = (token // (TOK // 2)).astype(F32)
    far = (token // (TOK // 4) % 2).astype(F32)

    def rows(*values):
        out = jnp.zeros((16, TOK), F32)
        for n, value in enumerate(values):
            out = jnp.where(feature == n, value, out)
        return out

    key = rows(low, 1 - low, far, 1 - far)
    query = -BLOCK * rows(
        last_row * (1 - low), last_row * low, last_col * (1 - far), last_col * far
    )
    return key.astype(BF), query.astype(BF)


def project_kernel(
    x0_ref, x1_ref, x2_ref, x3_ref, w_hbm_ref, after_ref,
    query_ref, key_ref, value_ref, unit_scale_ref, window_ref, w_qkv_ref, sems,
):
    copies = []
    for n in range(3):
        span = pl.ds(n * C, C)
        copies.append(
            pltpu.make_async_copy(w_hbm_ref.at[:, span], w_qkv_ref.at[:, span], sems.at[n])
        )
        copies[-1].start()
    x = jnp.concatenate([x0_ref[...], x1_ref[...], x2_ref[...], x3_ref[...]], axis=0)
    window_ref[...] = x
    for col in range(0, 3 * C, TOK):
        if col % C == 0:
            copies[col // C].wait()
        raw = dot(x, w_qkv_ref[:, col : col + TOK]).T
        if col < 2 * C:
            heads = raw.reshape(TOK // DIM, DIM, TOK)
            inv = lax.rsqrt(jnp.sum(heads * heads, axis=1, keepdims=True) + EPS_NORM)
            unit = (heads * inv).reshape(TOK, TOK)
            unit_scale_ref[col // DIM : (col + TOK) // DIM, :] = inv[:, 0, :]
            if col < C:
                query_ref[col : col + TOK, :] = unit
            else:
                key_ref[col - C : col - C + TOK, :] = unit
        else:
            value_ref[col - 2 * C : col - 2 * C + TOK, :] = raw.astype(BF)


def attention_kernel(
    rows, cols, query_ref, key_ref, value_ref, scale_ref, after_ref, after2_ref, after3_ref,
    att_ref, probs_ref,
):
    key_mask, query_mask = mask_features(*last_window(rows, cols))

    def head(h, carry):
        rows = head_rows(h)
        raw = dot(
            jnp.concatenate([key_ref[rows, :].astype(BF), key_mask], axis=0),
            jnp.concatenate([query_ref[rows, :].astype(BF), query_mask], axis=0),
            TN,
        )
        top = jnp.max(raw, axis=0, keepdims=True)
        expo = jnp.exp2((raw - top) * (scale_ref[h] * LOG2E))
        probs = expo * (1.0 / jnp.sum(expo, axis=0, keepdims=True))
        probs_ref[h] = probs
        att_ref[rows, :] = dot(probs.astype(BF), value_ref[rows, :], TT).T.astype(BF)
        return carry

    lax.fori_loop(0, HEADS, head, 0, unroll=8)


def norm_kernel(
    att_ref, g0_ref, g1_ref, g2_ref, g3_ref, w_proj_ref, gain_ref, after_ref,
    grad_mix_ref, grad_att_ref,
):
    g = jnp.concatenate([g0_ref[...], g1_ref[...], g2_ref[...], g3_ref[...]], axis=0)
    mixed = dot(att_ref[...], w_proj_ref[...], TN)
    center = mixed - jnp.mean(mixed, axis=-1, keepdims=True)
    inv_std = lax.rsqrt(jnp.mean(center * center, axis=-1, keepdims=True) + EPS_LN)
    normed = center * inv_std
    grad_norm = g.astype(F32) * gain_ref[...]
    grad_mix = inv_std * (
        grad_norm
        - jnp.mean(grad_norm, axis=-1, keepdims=True)
        - normed * jnp.mean(grad_norm * normed, axis=-1, keepdims=True)
    )
    grad_mix = grad_mix.astype(BF)
    grad_mix_ref[...] = grad_mix
    for row in range(0, C, TOK):
        grad_att_ref[row : row + TOK, :] = dot(
            w_proj_ref[row : row + TOK, :], grad_mix, NT
        ).astype(BF)


def value_kernel(probs_ref, grad_att_ref, after_ref, grad_value_ref):
    def head(h, carry):
        rows = head_rows(h)
        grad_value_ref[rows, :] = dot(
            grad_att_ref[rows, :], probs_ref[h].astype(BF), NT
        ).astype(BF)
        return carry

    lax.fori_loop(0, HEADS, head, 0, unroll=8)


def left_kernel(order_ref, att_ref, att2_ref, x_ref, x2_ref, after_ref, left_ref):
    @pl.when(core_index() == 0)
    def _():
        att = jnp.concatenate([att_ref[...], att2_ref[...]], axis=1)
        left_ref[...] = dot(order_ref[...], att).astype(BF)

    @pl.when(core_index() == 1)
    def _():
        x = jnp.concatenate([x_ref[...], x2_ref[...]], axis=0)
        left_ref[...] = dot(order_ref[...], x, NT).astype(BF)


def term_kernel(
    left_ref, grad_mix_ref, grad_mix2_ref, grad_value_ref, grad_value2_ref, *out_refs
):
    def write(col, term):
        for n, out_ref in enumerate(out_refs):
            out_ref[:, col : col + TOK] = term[n * TOK : n * TOK + TOK].astype(BF)

    left = left_ref[...]

    @pl.when(core_index() == 0)
    def _():
        grad_mix = jnp.concatenate([grad_mix_ref[...], grad_mix2_ref[...]], axis=0)
        for col in range(0, C, TOK):
            write(col, dot(left, grad_mix[:, col : col + TOK]))

    @pl.when(core_index() == 1)
    def _():
        grad_value = jnp.concatenate([grad_value_ref[...], grad_value2_ref[...]], axis=1)
        for col in range(0, C, TOK):
            write(col, dot(left, grad_value[col : col + TOK, :], NT))


def sum_kernel(own_ref, *refs):
    total = own_ref[...].astype(F32)
    for other in refs[:3]:
        total += other[...].astype(F32)
    total = total.astype(BF)
    size = total.shape[0] // len(refs[3:])
    for n, out_ref in enumerate(refs[3:]):
        out_ref[...] = total[n * size : n * size + size]


def score_kernel(
    first, count, probs_ref, grad_att_ref, query_ref, key_ref, value_ref, unit_scale_ref,
    scale_ref, after_ref, grad_query_ref, grad_key_ref, grad_score_ref,
):
    def scores(n, carry):
        h = n + first
        rows = head_rows(h)
        probs = probs_ref[h]
        grad_prob = dot(value_ref[rows, :], grad_att_ref[rows, :], TN)
        mean = jnp.sum(grad_prob * probs, axis=0, keepdims=True)
        grad_score_ref[n] = (scale_ref[h] * (probs * (grad_prob - mean))).astype(BF)
        return carry

    def units(n, carry):
        h = n + first
        rows, out_rows = head_rows(h), head_rows(n)
        query = query_ref[rows, :]
        key = key_ref[rows, :]
        grad_score = grad_score_ref[n]
        grad_query = dot(key.astype(BF), grad_score)
        grad_key = dot(grad_score, query.astype(BF), NT).T
        grad_query = unit_scale_ref[pl.ds(h, 1), :] * (
            grad_query - query * jnp.sum(grad_query * query, axis=0, keepdims=True)
        )
        grad_key = unit_scale_ref[pl.ds(h + HEADS, 1), :] * (
            grad_key - key * jnp.sum(grad_key * key, axis=0, keepdims=True)
        )
        grad_query_ref[out_rows, :] = grad_query.astype(BF)
        grad_key_ref[out_rows, :] = grad_key.astype(BF)
        return carry

    lax.fori_loop(0, count, scores, 0, unroll=8)
    lax.fori_loop(0, count, units, 0, unroll=16)


def input_kernel(*refs):
    parts, w_qkv_ref, out_refs = refs[:-5], refs[-5], refs[-4:]
    for row in range(0, C, TOK):
        total, col = 0.0, 0
        for part in parts:
            size = part.shape[0]
            total += dot(w_qkv_ref[row : row + TOK, col : col + size], part[...])
            col += size
        total = total.T.astype(BF)
        for n, out_ref in enumerate(out_refs):
            out_ref[:, row : row + TOK] = total[n * 64 : n * 64 + 64]


VM = pl.BlockSpec(memory_space=pltpu.VMEM)
ANY = pl.BlockSpec(memory_space=pl.ANY)
SM = pl.BlockSpec(memory_space=pltpu.SMEM)


def shape(dims, kind):
    return jax.ShapeDtypeStruct(dims, kind)


def call(kernel, outs, ins, micros, name, limit, scratch=()):
    return pl.pallas_call(
        kernel,
        out_shape=outs,
        in_specs=ins,
        out_specs=jax.tree.map(lambda _: VM, outs),
        scratch_shapes=scratch,
        compiler_params=pltpu.CompilerParams(vmem_limit_bytes=limit * MIB),
        cost_estimate=pl.CostEstimate(
            flops=int(micros * 11 * 10**8), bytes_accessed=MIB, transcendentals=0
        ),
        name=name,
    )


def project(quads, w_qkv, after):
    flat = shape((C, TOK), F32)
    outs = (
        flat, flat, shape((C, TOK), BF), shape((2 * HEADS, TOK), F32), shape((TOK, C), BF),
    )
    scratch = [pltpu.VMEM((C, 3 * C), BF), pltpu.SemaphoreType.DMA((3,))]
    ins = [VM] * 4 + [pl.BlockSpec(memory_space=pltpu.HBM), ANY]
    return call(project_kernel, outs, ins, 4, "project_part", 24, scratch)(
        *quads, pltpu.with_memory_space_constraint(w_qkv, pltpu.HBM), after
    )


def attention(rows, cols, *args):
    outs = (shape((C, TOK), BF), shape((HEADS, TOK, TOK), F32))
    kernel = functools.partial(attention_kernel, rows, cols)
    return call(kernel, outs, [VM] * 3 + [SM] + [ANY] * 3, 6, "attention_part", 16)(*args)


def output_norm(att, quads, w_proj, gain, after):
    outs = (shape((TOK, C), BF), shape((C, TOK), BF))
    return call(norm_kernel, outs, [VM] * 7 + [ANY], 2, "norm_part", 16)(
        att, *quads, w_proj, gain, after
    )


def value_grads(*args):
    ins = [VM] * 2 + [ANY]
    return call(value_kernel, shape((C, TOK), BF), ins, 2, "value_part", 16)(*args)


def left_rows(*args):
    ins = [VM] * 5 + [ANY]
    return call(left_kernel, shape((C, 2 * TOK), BF), ins, 1.2, "left_rows", 24)(*args)


def weight_terms(*args):
    outs = (shape((TOK, C), BF),) * 4
    return call(term_kernel, outs, [VM] * 5, 1.3, "weight_terms", 24)(*args)


def score_grads(first, count, *args):
    outs = (shape((count * DIM, TOK), BF),) * 2
    scratch = [pltpu.VMEM((count, TOK, TOK), BF)]
    kernel = functools.partial(score_kernel, first, count)
    ins = [VM] * 6 + [SM, ANY]
    return call(kernel, outs, ins, 0.3, "score_part", 16, scratch)(*args)


def block_sums(count, *blocks):
    outs = (shape((64, C), BF),) * count
    return call(sum_kernel, outs, [VM] * 4, 0.5, "block_sums", 16)(*blocks)


def input_grad(parts, w_qkv):
    outs = (shape((TOK // 4, C), BF),) * 4
    return call(input_kernel, outs, [VM] * (len(parts) + 1), 0.2, "input_part", 24)(*parts, w_qkv)


def passed(array, d_row, d_col, rows, cols):
    pairs = [
        (r * cols + c, (r + d_row) % rows * cols + (c + d_col) % cols)
        for r in range(rows)
        for c in range(cols)
    ]
    return lax.ppermute(array, ("row", "col"), pairs)


def window(array, rows, cols):
    def quad(r, c):
        return array[r : r + HALF, c : c + HALF].reshape(TOK // 4, C)

    return (
        quad(HALF, HALF),
        passed(quad(HALF, 0), 0, -1, rows, cols),
        passed(quad(0, HALF), -1, 0, rows, cols),
        passed(quad(0, 0), -1, -1, rows, cols),
    )


def line(x, y, z, core):
    return ((z * 2 + x // 2) * 2 + core) * 8 + y * 2 + x % 2


CHIPS = [(x, y, z, core) for x in range(4) for y in range(4) for z in range(8) for core in range(2)]
BOTH = ("row", "col")


def other_core(array):
    pairs = [(line(x, y, z, core), line(x, y, z, 1 - core)) for x, y, z, core in CHIPS]
    return lax.ppermute(array, BOTH, pairs)


def moved(array, stage, by):
    pairs = []
    for x, y, z, core in CHIPS:
        to = ((x + by) % 4, y) if core == stage else (x, (y + by) % 4)
        pairs.append((line(x, y, z, core), line(*to, z, core)))
    return lax.ppermute(array, BOTH, pairs)


def gathered(blocks, stage):
    far = moved(blocks[2], stage, 2)
    return far, moved(blocks[1], stage, 1), moved(blocks[3], stage, -1)


def row_order():
    place = jnp.arange(C, dtype=jnp.int32)
    a, b, z, far, row = place // 256, place // 64 % 4, place // 8 % 8, place // 4 % 2, place % 4
    r, c = lax.axis_index("row"), lax.axis_index("col")
    core = r % 2
    dx, dy = jnp.where(core == 0, a, b), jnp.where(core == 0, b, a)
    x = (r // 2 % 2 * 2 + c % 2 + dx) % 4
    y = (c // 2 + dy) % 4
    source = z * 128 + x // 2 * 64 + (core + far) % 2 * 32 + y * 8 + x % 2 * 4 + row
    return (source[:, None] == jnp.arange(C, dtype=jnp.int32)[None, :]).astype(BF)


def group_sum(blocks, groups):
    got = lax.all_to_all(blocks, BOTH, 0, 0, axis_index_groups=groups, tiled=True)
    return jnp.sum(got.astype(F32), axis=0)


def z_sum(blocks):
    groups = [
        [line(x, y, z, core) for z in range(8)]
        for x in range(4)
        for y in range(4)
        for core in range(2)
    ]
    return group_sum(blocks, groups)


def per_device(tokens, grad_out, w_qkv, w_proj, norm_gain, logit_scale):
    rows, cols = lax.axis_size("row"), lax.axis_size("col")
    x = window(tokens, rows, cols)
    g = window(grad_out, rows, cols)
    order = row_order()
    query, key, value, unit_scale, tokens_win = project(x, w_qkv, order)
    att, probs = attention(rows, cols, query, key, value, logit_scale, *g[1:])
    tokens_win2, att2 = other_core(tokens_win), other_core(att)
    grad_mix, grad_att = output_norm(att, g, w_proj, norm_gain.reshape(1, C), tokens_win2)
    grad_value = value_grads(probs, grad_att, att2)
    grad_mix2, grad_value2 = other_core(grad_mix), other_core(grad_value)
    left = left_rows(order, att, att2, tokens_win, tokens_win2, grad_value)
    blocks = weight_terms(left, grad_mix, grad_mix2, grad_value, grad_value2)
    others = gathered(blocks, 0)
    grads = score_grads(
        0, HEADS, probs, grad_att, query, key, value, unit_scale, logit_scale, blocks[0]
    )
    parts = [*grads, grad_value]
    grad_input = input_grad(parts, w_qkv)
    grad_input, others = lax.optimization_barrier((grad_input, others))
    blocks = block_sums(4, blocks[0], *others)
    others = gathered(blocks, 1)
    terms, grad_input = lax.optimization_barrier(((blocks[0], *others), grad_input))
    (terms,) = block_sums(1, *terms)
    terms = z_sum(terms.reshape(8, 8, C))
    kept, got = terms[:4], other_core(terms[4:])
    first = lax.axis_index("row") % 2 == 0
    proj_part, value_part = jnp.where(first, kept, got), jnp.where(first, got, kept)
    back = jnp.stack(
        [
            passed(grad_input[3], 1, 1, rows, cols),
            passed(grad_input[2], 1, 0, rows, cols),
            passed(grad_input[1], 0, 1, rows, cols),
            grad_input[0],
        ]
    )
    back = back.reshape(2, 2, HALF, HALF, C).transpose(0, 2, 1, 3, 4).reshape(WIN, WIN, C)
    grad_tokens = (grad_out.astype(F32) + back.astype(F32)).astype(BF)
    return (grad_tokens, value_part, proj_part)


def solution(mesh):
    in_specs = (P("row", "col", None), P("row", "col", None), P(), P(), P(), P())
    out_specs = (P("row", "col", None), P(("row", "col"), None), P(("row", "col"), None))
    return jax.shard_map(
        per_device, mesh=mesh, in_specs=in_specs, out_specs=out_specs, check_vma=False
    )
```

```python
import functools
import math

import jax
import jax.numpy as jnp
from jax import lax
from jax.experimental import pallas as pl
from jax.experimental.pallas import tpu as pltpu
from jax.sharding import PartitionSpec as P

HEADS = 32
WIN = 16
HALF = WIN // 2
DIM = 32
TOK = WIN * WIN
C = 1024
EPS_NORM = 1e-06
EPS_LN = 1e-05
LOG2E = math.log2(math.e)
BLOCK = 2.0**20
BF = jnp.bfloat16
F32 = jnp.float32
MIB = 2**20


def dot(left, right, dims=((1,), (0,))):
    return lax.dot_general(left, right, (dims, ((), ())), preferred_element_type=F32)


TN = ((0,), (0,))
NT = ((1,), (1,))
TT = ((0,), (1,))


def head_rows(h):
    return pl.ds(pl.multiple_of(h * DIM, DIM), DIM)


def core_index():
    return lax.rem(lax.axis_index("row"), 2)


def last_window(rows, cols):
    last_row = (lax.axis_index("row") == rows - 1).astype(F32)
    last_col = (lax.axis_index("col") == cols - 1).astype(F32)
    return last_row, last_col


def mask_features(last_row, last_col):
    feature = lax.broadcasted_iota(jnp.int32, (16, TOK), 0)
    token = lax.broadcasted_iota(jnp.int32, (16, TOK), 1)
    low = (token // (TOK // 2)).astype(F32)
    far = (token // (TOK // 4) % 2).astype(F32)

    def rows(*values):
        out = jnp.zeros((16, TOK), F32)
        for n, value in enumerate(values):
            out = jnp.where(feature == n, value, out)
        return out

    key = rows(low, 1 - low, far, 1 - far)
    query = -BLOCK * rows(
        last_row * (1 - low), last_row * low, last_col * (1 - far), last_col * far
    )
    return key.astype(BF), query.astype(BF)


def project_kernel(
    x0_ref, x1_ref, x2_ref, x3_ref, w_hbm_ref, after_ref,
    query_ref, key_ref, value_ref, unit_scale_ref, window_ref, w_qkv_ref, sems,
):
    copies = []
    for n in range(3):
        span = pl.ds(n * C, C)
        copies.append(
            pltpu.make_async_copy(w_hbm_ref.at[:, span], w_qkv_ref.at[:, span], sems.at[n])
        )
        copies[-1].start()
    x = jnp.concatenate([x0_ref[...], x1_ref[...], x2_ref[...], x3_ref[...]], axis=0)
    window_ref[...] = x
    for col in range(0, 3 * C, TOK):
        if col % C == 0:
            copies[col // C].wait()
        raw = dot(x, w_qkv_ref[:, col : col + TOK]).T
        if col < 2 * C:
            heads = raw.reshape(TOK // DIM, DIM, TOK)
            inv = lax.rsqrt(jnp.sum(heads * heads, axis=1, keepdims=True) + EPS_NORM)
            unit = (heads * inv).reshape(TOK, TOK)
            unit_scale_ref[col // DIM : (col + TOK) // DIM, :] = inv[:, 0, :]
            if col < C:
                query_ref[col : col + TOK, :] = unit
            else:
                key_ref[col - C : col - C + TOK, :] = unit
        else:
            value_ref[col - 2 * C : col - 2 * C + TOK, :] = raw.astype(BF)


def attention_kernel(
    rows, cols, query_ref, key_ref, value_ref, scale_ref, after_ref, after2_ref, after3_ref,
    att_ref, probs_ref,
):
    key_mask, query_mask = mask_features(*last_window(rows, cols))

    def head(h, carry):
        rows = head_rows(h)
        raw = dot(
            jnp.concatenate([key_ref[rows, :].astype(BF), key_mask], axis=0),
            jnp.concatenate([query_ref[rows, :].astype(BF), query_mask], axis=0),
            TN,
        )
        top = jnp.max(raw, axis=0, keepdims=True)
        expo = jnp.exp2((raw - top) * (scale_ref[h] * LOG2E))
        probs = expo * (1.0 / jnp.sum(expo, axis=0, keepdims=True))
        probs_ref[h] = probs
        att_ref[rows, :] = dot(probs.astype(BF), value_ref[rows, :], TT).T.astype(BF)
        return carry

    lax.fori_loop(0, HEADS, head, 0, unroll=HEADS)


def norm_kernel(
    att_ref, g0_ref, g1_ref, g2_ref, g3_ref, w_proj_ref, gain_ref, after_ref,
    grad_mix_ref, grad_att_ref,
):
    g = jnp.concatenate([g0_ref[...], g1_ref[...], g2_ref[...], g3_ref[...]], axis=0)
    mixed = dot(att_ref[...], w_proj_ref[...], TN)
    center = mixed - jnp.mean(mixed, axis=-1, keepdims=True)
    inv_std = lax.rsqrt(jnp.mean(center * center, axis=-1, keepdims=True) + EPS_LN)
    normed = center * inv_std
    grad_norm = g.astype(F32) * gain_ref[...]
    grad_mix = inv_std * (
        grad_norm
        - jnp.mean(grad_norm, axis=-1, keepdims=True)
        - normed * jnp.mean(grad_norm * normed, axis=-1, keepdims=True)
    )
    grad_mix = grad_mix.astype(BF)
    grad_mix_ref[...] = grad_mix
    for row in range(0, C, TOK):
        grad_att_ref[row : row + TOK, :] = dot(
            w_proj_ref[row : row + TOK, :], grad_mix, NT
        ).astype(BF)


def value_kernel(probs_ref, grad_att_ref, after_ref, grad_value_ref):
    def head(h, carry):
        rows = head_rows(h)
        grad_value_ref[rows, :] = dot(
            grad_att_ref[rows, :], probs_ref[h].astype(BF), NT
        ).astype(BF)
        return carry

    lax.fori_loop(0, HEADS, head, 0, unroll=HEADS)


def left_kernel(order_ref, att_ref, att2_ref, x_ref, x2_ref, after_ref, left_ref):
    @pl.when(core_index() == 0)
    def _():
        att = jnp.concatenate([att_ref[...], att2_ref[...]], axis=1)
        left_ref[...] = dot(order_ref[...], att).astype(BF)

    @pl.when(core_index() == 1)
    def _():
        x = jnp.concatenate([x_ref[...], x2_ref[...]], axis=0)
        left_ref[...] = dot(order_ref[...], x, NT).astype(BF)


def term_kernel(
    spans, left_ref, grad_mix_ref, grad_mix2_ref, grad_value_ref, grad_value2_ref, *out_refs
):
    def write(col, term):
        for n, out_ref in enumerate(out_refs):
            out_ref[:, col : col + TOK] = term[n * TOK : n * TOK + TOK].astype(BF)

    left = jnp.concatenate([left_ref[a:b, :] for a, b in spans], axis=0)

    @pl.when(core_index() == 0)
    def _():
        grad_mix = jnp.concatenate([grad_mix_ref[...], grad_mix2_ref[...]], axis=0)
        for col in range(0, C, TOK):
            write(col, dot(left, grad_mix[:, col : col + TOK]))

    @pl.when(core_index() == 1)
    def _():
        grad_value = jnp.concatenate([grad_value_ref[...], grad_value2_ref[...]], axis=1)
        for col in range(0, C, TOK):
            write(col, dot(left, grad_value[col : col + TOK, :], NT))


def sum_kernel(own_ref, *refs):
    total = own_ref[...].astype(F32)
    for other in refs[:3]:
        total += other[...].astype(F32)
    total = total.astype(BF)
    size = total.shape[0] // len(refs[3:])
    for n, out_ref in enumerate(refs[3:]):
        out_ref[...] = total[n * size : n * size + size]


def score_kernel(
    first, count, probs_ref, grad_att_ref, query_ref, key_ref, value_ref, unit_scale_ref,
    scale_ref, after_ref, grad_query_ref, grad_key_ref, grad_score_ref,
):
    def scores(n, carry):
        h = n + first
        rows = head_rows(h)
        probs = probs_ref[h]
        grad_prob = dot(value_ref[rows, :], grad_att_ref[rows, :], TN)
        mean = jnp.sum(grad_prob * probs, axis=0, keepdims=True)
        grad_score_ref[n] = (scale_ref[h] * (probs * (grad_prob - mean))).astype(BF)
        return carry

    def units(n, carry):
        h = n + first
        rows, out_rows = head_rows(h), head_rows(n)
        query = query_ref[rows, :]
        key = key_ref[rows, :]
        grad_score = grad_score_ref[n]
        grad_query = dot(key.astype(BF), grad_score)
        grad_key = dot(grad_score, query.astype(BF), NT).T
        grad_query = unit_scale_ref[pl.ds(h, 1), :] * (
            grad_query - query * jnp.sum(grad_query * query, axis=0, keepdims=True)
        )
        grad_key = unit_scale_ref[pl.ds(h + HEADS, 1), :] * (
            grad_key - key * jnp.sum(grad_key * key, axis=0, keepdims=True)
        )
        grad_query_ref[out_rows, :] = grad_query.astype(BF)
        grad_key_ref[out_rows, :] = grad_key.astype(BF)
        return carry

    lax.fori_loop(0, count, scores, 0, unroll=8)
    lax.fori_loop(0, count, units, 0, unroll=16)


def input_kernel(*refs):
    parts, w_qkv_ref, out_refs = refs[:-5], refs[-5], refs[-4:]
    for row in range(0, C, TOK):
        total, col = 0.0, 0
        for part in parts:
            size = part.shape[0]
            total += dot(w_qkv_ref[row : row + TOK, col : col + size], part[...])
            col += size
        total = total.T.astype(BF)
        for n, out_ref in enumerate(out_refs):
            out_ref[:, row : row + TOK] = total[n * 64 : n * 64 + 64]


VM = pl.BlockSpec(memory_space=pltpu.VMEM)
ANY = pl.BlockSpec(memory_space=pl.ANY)
SM = pl.BlockSpec(memory_space=pltpu.SMEM)


def shape(dims, kind):
    return jax.ShapeDtypeStruct(dims, kind)


def call(kernel, outs, ins, micros, name, limit, scratch=()):
    return pl.pallas_call(
        kernel,
        out_shape=outs,
        in_specs=ins,
        out_specs=jax.tree.map(lambda _: VM, outs),
        scratch_shapes=scratch,
        compiler_params=pltpu.CompilerParams(vmem_limit_bytes=limit * MIB),
        cost_estimate=pl.CostEstimate(
            flops=int(micros * 11 * 10**8), bytes_accessed=MIB, transcendentals=0
        ),
        name=name,
    )


def project(quads, w_qkv, after):
    flat = shape((C, TOK), F32)
    outs = (
        flat, flat, shape((C, TOK), BF), shape((2 * HEADS, TOK), F32), shape((TOK, C), BF),
    )
    scratch = [pltpu.VMEM((C, 3 * C), BF), pltpu.SemaphoreType.DMA((3,))]
    ins = [VM] * 4 + [pl.BlockSpec(memory_space=pltpu.HBM), ANY]
    return call(project_kernel, outs, ins, 4, "project_part", 24, scratch)(
        *quads, pltpu.with_memory_space_constraint(w_qkv, pltpu.HBM), after
    )


def attention(rows, cols, *args):
    outs = (shape((C, TOK), BF), shape((HEADS, TOK, TOK), F32))
    kernel = functools.partial(attention_kernel, rows, cols)
    return call(kernel, outs, [VM] * 3 + [SM] + [ANY] * 3, 6, "attention_part", 16)(*args)


def output_norm(att, quads, w_proj, gain, after):
    outs = (shape((TOK, C), BF), shape((C, TOK), BF))
    return call(norm_kernel, outs, [VM] * 7 + [ANY], 2, "norm_part", 16)(
        att, *quads, w_proj, gain, after
    )


def value_grads(*args):
    ins = [VM] * 2 + [ANY]
    return call(value_kernel, shape((C, TOK), BF), ins, 2, "value_part", 16)(*args)


def left_rows(*args):
    ins = [VM] * 5 + [ANY]
    return call(left_kernel, shape((C, 2 * TOK), BF), ins, 1.2, "left_rows", 24)(*args)


def weight_terms(*args):
    def part(*spans):
        outs = (shape((TOK, C), BF),) * (sum(b - a for a, b in spans) // TOK)
        kernel = functools.partial(term_kernel, spans)
        return call(kernel, outs, [VM] * 5, 0.6, "weight_terms", 24)(*args)

    (far,) = part((2 * TOK, 3 * TOK))
    own, one, three = part((0, 2 * TOK), (3 * TOK, 4 * TOK))
    return own, one, far, three


def score_grads(first, count, *args):
    outs = (shape((count * DIM, TOK), BF),) * 2
    scratch = [pltpu.VMEM((count, TOK, TOK), BF)]
    kernel = functools.partial(score_kernel, first, count)
    ins = [VM] * 6 + [SM, ANY]
    return call(kernel, outs, ins, 0.3, "score_part", 16, scratch)(*args)


def block_sums(count, *blocks):
    outs = (shape((64, C), BF),) * count
    return call(sum_kernel, outs, [VM] * 4, 0.5, "block_sums", 16)(*blocks)


def input_grad(parts, w_qkv):
    outs = (shape((TOK // 4, C), BF),) * 4
    return call(input_kernel, outs, [VM] * (len(parts) + 1), 0.2, "input_part", 24)(*parts, w_qkv)


def passed(array, d_row, d_col, rows, cols):
    pairs = [
        (r * cols + c, (r + d_row) % rows * cols + (c + d_col) % cols)
        for r in range(rows)
        for c in range(cols)
    ]
    return lax.ppermute(array, ("row", "col"), pairs)


def window(array, rows, cols):
    def quad(r, c):
        return array[r : r + HALF, c : c + HALF].reshape(TOK // 4, C)

    return (
        quad(HALF, HALF),
        passed(quad(HALF, 0), 0, -1, rows, cols),
        passed(quad(0, HALF), -1, 0, rows, cols),
        passed(quad(0, 0), -1, -1, rows, cols),
    )


def line(x, y, z, core):
    return ((z * 2 + x // 2) * 2 + core) * 8 + y * 2 + x % 2


CHIPS = [(x, y, z, core) for x in range(4) for y in range(4) for z in range(8) for core in range(2)]
BOTH = ("row", "col")


def other_core(array):
    pairs = [(line(x, y, z, core), line(x, y, z, 1 - core)) for x, y, z, core in CHIPS]
    return lax.ppermute(array, BOTH, pairs)


def moved(array, stage, by):
    pairs = []
    for x, y, z, core in CHIPS:
        to = ((x + by) % 4, y) if core == stage else (x, (y + by) % 4)
        pairs.append((line(x, y, z, core), line(*to, z, core)))
    return lax.ppermute(array, BOTH, pairs)


def gathered(blocks, stage):
    far = moved(blocks[2], stage, 2)
    return far, moved(blocks[1], stage, 1), moved(blocks[3], stage, -1)


def row_order():
    place = jnp.arange(C, dtype=jnp.int32)
    a, b, z, far, row = place // 256, place // 64 % 4, place // 8 % 8, place // 4 % 2, place % 4
    r, c = lax.axis_index("row"), lax.axis_index("col")
    core = r % 2
    dx, dy = jnp.where(core == 0, a, b), jnp.where(core == 0, b, a)
    x = (r // 2 % 2 * 2 + c % 2 + dx) % 4
    y = (c // 2 + dy) % 4
    source = z * 128 + x // 2 * 64 + (core + far) % 2 * 32 + y * 8 + x % 2 * 4 + row
    return (source[:, None] == jnp.arange(C, dtype=jnp.int32)[None, :]).astype(BF)


def group_sum(blocks, groups):
    got = lax.all_to_all(blocks, BOTH, 0, 0, axis_index_groups=groups, tiled=True)
    return jnp.sum(got.astype(F32), axis=0)


def z_sum(blocks):
    groups = [
        [line(x, y, z, core) for z in range(8)]
        for x in range(4)
        for y in range(4)
        for core in range(2)
    ]
    return group_sum(blocks, groups)


def per_device(tokens, grad_out, w_qkv, w_proj, norm_gain, logit_scale):
    rows, cols = lax.axis_size("row"), lax.axis_size("col")
    x = window(tokens, rows, cols)
    g = window(grad_out, rows, cols)
    order = row_order()
    query, key, value, unit_scale, tokens_win = project(x, w_qkv, order)
    att, probs = attention(rows, cols, query, key, value, logit_scale, *g[1:])
    tokens_win2, att2 = other_core(tokens_win), other_core(att)
    grad_mix, grad_att = output_norm(att, g, w_proj, norm_gain.reshape(1, C), tokens_win2)
    grad_value = value_grads(probs, grad_att, att2)
    grad_mix2, grad_value2 = other_core(grad_mix), other_core(grad_value)
    left = left_rows(order, att, att2, tokens_win, tokens_win2, grad_value)
    blocks = weight_terms(left, grad_mix, grad_mix2, grad_value, grad_value2)
    others = gathered(blocks, 0)
    grads = score_grads(
        0, HEADS, probs, grad_att, query, key, value, unit_scale, logit_scale, blocks[0]
    )
    parts = [*grads, grad_value]
    grad_input = input_grad(parts, w_qkv)
    grad_input, others = lax.optimization_barrier((grad_input, others))
    blocks = block_sums(4, blocks[0], *others)
    blocks, grad_input = lax.optimization_barrier((blocks, grad_input))
    others = gathered(blocks, 1)
    (terms,) = block_sums(1, blocks[0], *others)
    terms = z_sum(terms.reshape(8, 8, C))
    kept, got = terms[:4], other_core(terms[4:])
    first = lax.axis_index("row") % 2 == 0
    proj_part, value_part = jnp.where(first, kept, got), jnp.where(first, got, kept)
    back = jnp.stack(
        [
            passed(grad_input[3], 1, 1, rows, cols),
            passed(grad_input[2], 1, 0, rows, cols),
            passed(grad_input[1], 0, 1, rows, cols),
            grad_input[0],
        ]
    )
    back = back.reshape(2, 2, HALF, HALF, C).transpose(0, 2, 1, 3, 4).reshape(WIN, WIN, C)
    grad_tokens = (grad_out.astype(F32) + back.astype(F32)).astype(BF)
    return (grad_tokens, value_part, proj_part)


def solution(mesh):
    in_specs = (P("row", "col", None), P("row", "col", None), P(), P(), P(), P())
    out_specs = (P("row", "col", None), P(("row", "col"), None), P(("row", "col"), None))
    return jax.shard_map(
        per_device, mesh=mesh, in_specs=in_specs, out_specs=out_specs, check_vma=False
    )
```

```python
import functools
import math

import jax
import jax.numpy as jnp
from jax import lax
from jax.experimental import pallas as pl
from jax.experimental.pallas import tpu as pltpu
from jax.sharding import PartitionSpec as P

HEADS = 32
WIN = 16
HALF = WIN // 2
DIM = 32
TOK = WIN * WIN
C = 1024
EPS_NORM = 1e-06
EPS_LN = 1e-05
LOG2E = math.log2(math.e)
BLOCK = 2.0**20
BF = jnp.bfloat16
F32 = jnp.float32
MIB = 2**20


def dot(left, right, dims=((1,), (0,))):
    return lax.dot_general(left, right, (dims, ((), ())), preferred_element_type=F32)


TN = ((0,), (0,))
NT = ((1,), (1,))
TT = ((0,), (1,))


def head_rows(h):
    return pl.ds(pl.multiple_of(h * DIM, DIM), DIM)


def core_index():
    return lax.rem(lax.axis_index("row"), 2)


def last_window(rows, cols):
    last_row = (lax.axis_index("row") == rows - 1).astype(F32)
    last_col = (lax.axis_index("col") == cols - 1).astype(F32)
    return last_row, last_col


def mask_features(last_row, last_col):
    feature = lax.broadcasted_iota(jnp.int32, (16, TOK), 0)
    token = lax.broadcasted_iota(jnp.int32, (16, TOK), 1)
    low = (token // (TOK // 2)).astype(F32)
    far = (token // (TOK // 4) % 2).astype(F32)

    def rows(*values):
        out = jnp.zeros((16, TOK), F32)
        for n, value in enumerate(values):
            out = jnp.where(feature == n, value, out)
        return out

    key = rows(low, 1 - low, far, 1 - far)
    query = -BLOCK * rows(
        last_row * (1 - low), last_row * low, last_col * (1 - far), last_col * far
    )
    return key.astype(BF), query.astype(BF)


def project_kernel(
    x0_ref, x1_ref, x2_ref, x3_ref, w_hbm_ref, after_ref,
    query_ref, key_ref, value_ref, unit_scale_ref, window_ref, w_qkv_ref, sems,
):
    copies = []
    for n in range(3):
        span = pl.ds(n * C, C)
        copies.append(
            pltpu.make_async_copy(w_hbm_ref.at[:, span], w_qkv_ref.at[:, span], sems.at[n])
        )
        copies[-1].start()
    x = jnp.concatenate([x0_ref[...], x1_ref[...], x2_ref[...], x3_ref[...]], axis=0)
    window_ref[...] = x
    for col in range(0, 3 * C, TOK):
        if col % C == 0:
            copies[col // C].wait()
        raw = dot(x, w_qkv_ref[:, col : col + TOK]).T
        if col < 2 * C:
            heads = raw.reshape(TOK // DIM, DIM, TOK)
            inv = lax.rsqrt(jnp.sum(heads * heads, axis=1, keepdims=True) + EPS_NORM)
            unit = (heads * inv).reshape(TOK, TOK)
            unit_scale_ref[col // DIM : (col + TOK) // DIM, :] = inv[:, 0, :]
            if col < C:
                query_ref[col : col + TOK, :] = unit
            else:
                key_ref[col - C : col - C + TOK, :] = unit
        else:
            value_ref[col - 2 * C : col - 2 * C + TOK, :] = raw.astype(BF)


def attention_kernel(
    rows, cols, query_ref, key_ref, value_ref, scale_ref, after_ref, after2_ref, after3_ref,
    att_ref, probs_ref,
):
    key_mask, query_mask = mask_features(*last_window(rows, cols))

    def head(h, carry):
        rows = head_rows(h)
        raw = dot(
            jnp.concatenate([key_ref[rows, :].astype(BF), key_mask], axis=0),
            jnp.concatenate([query_ref[rows, :].astype(BF), query_mask], axis=0),
            TN,
        )
        top = jnp.max(raw, axis=0, keepdims=True)
        expo = jnp.exp2((raw - top) * (scale_ref[h] * LOG2E))
        probs = expo * (1.0 / jnp.sum(expo, axis=0, keepdims=True))
        probs_ref[h] = probs
        att_ref[rows, :] = dot(probs.astype(BF), value_ref[rows, :], TT).T.astype(BF)
        return carry

    lax.fori_loop(0, HEADS, head, 0, unroll=HEADS)


def norm_kernel(
    att_ref, g0_ref, g1_ref, g2_ref, g3_ref, w_proj_ref, gain_ref, after_ref,
    grad_mix_ref, grad_att_ref,
):
    g = jnp.concatenate([g0_ref[...], g1_ref[...], g2_ref[...], g3_ref[...]], axis=0)
    mixed = dot(att_ref[...], w_proj_ref[...], TN)
    center = mixed - jnp.mean(mixed, axis=-1, keepdims=True)
    inv_std = lax.rsqrt(jnp.mean(center * center, axis=-1, keepdims=True) + EPS_LN)
    normed = center * inv_std
    grad_norm = g.astype(F32) * gain_ref[...]
    grad_mix = inv_std * (
        grad_norm
        - jnp.mean(grad_norm, axis=-1, keepdims=True)
        - normed * jnp.mean(grad_norm * normed, axis=-1, keepdims=True)
    )
    grad_mix = grad_mix.astype(BF)
    grad_mix_ref[...] = grad_mix
    for row in range(0, C, TOK):
        grad_att_ref[row : row + TOK, :] = dot(
            w_proj_ref[row : row + TOK, :], grad_mix, NT
        ).astype(BF)


def value_kernel(probs_ref, grad_att_ref, after_ref, grad_value_ref):
    def head(h, carry):
        rows = head_rows(h)
        grad_value_ref[rows, :] = dot(
            grad_att_ref[rows, :], probs_ref[h].astype(BF), NT
        ).astype(BF)
        return carry

    lax.fori_loop(0, HEADS, head, 0, unroll=HEADS)


def left_kernel(order_ref, att_ref, att2_ref, x_ref, x2_ref, after_ref, left_ref):
    @pl.when(core_index() == 0)
    def _():
        att = jnp.concatenate([att_ref[...], att2_ref[...]], axis=1)
        left_ref[...] = dot(order_ref[...], att).astype(BF)

    @pl.when(core_index() == 1)
    def _():
        x = jnp.concatenate([x_ref[...], x2_ref[...]], axis=0)
        left_ref[...] = dot(order_ref[...], x, NT).astype(BF)


def term_kernel(
    spans, left_ref, grad_mix_ref, grad_mix2_ref, grad_value_ref, grad_value2_ref, *out_refs
):
    def write(col, term):
        for n, out_ref in enumerate(out_refs):
            out_ref[:, col : col + TOK] = term[n * TOK : n * TOK + TOK].astype(BF)

    left = jnp.concatenate([left_ref[a:b, :] for a, b in spans], axis=0)

    @pl.when(core_index() == 0)
    def _():
        grad_mix = jnp.concatenate([grad_mix_ref[...], grad_mix2_ref[...]], axis=0)
        for col in range(0, C, TOK):
            write(col, dot(left, grad_mix[:, col : col + TOK]))

    @pl.when(core_index() == 1)
    def _():
        grad_value = jnp.concatenate([grad_value_ref[...], grad_value2_ref[...]], axis=1)
        for col in range(0, C, TOK):
            write(col, dot(left, grad_value[col : col + TOK, :], NT))


def sum_kernel(own_ref, *refs):
    total = own_ref[...].astype(F32)
    for other in refs[:3]:
        total += other[...].astype(F32)
    total = total.astype(BF)
    size = total.shape[0] // len(refs[3:])
    for n, out_ref in enumerate(refs[3:]):
        out_ref[...] = total[n * size : n * size + size]


def score_kernel(
    first, count, probs_ref, grad_att_ref, query_ref, key_ref, value_ref, unit_scale_ref,
    scale_ref, after_ref, grad_query_ref, grad_key_ref, grad_score_ref,
):
    def scores(n, carry):
        h = n + first
        rows = head_rows(h)
        probs = probs_ref[h]
        grad_prob = dot(value_ref[rows, :], grad_att_ref[rows, :], TN)
        mean = jnp.sum(grad_prob * probs, axis=0, keepdims=True)
        grad_score_ref[n] = (scale_ref[h] * (probs * (grad_prob - mean))).astype(BF)
        return carry

    def units(n, carry):
        h = n + first
        rows, out_rows = head_rows(h), head_rows(n)
        query = query_ref[rows, :]
        key = key_ref[rows, :]
        grad_score = grad_score_ref[n]
        grad_query = dot(key.astype(BF), grad_score)
        grad_key = dot(grad_score, query.astype(BF), NT).T
        grad_query = unit_scale_ref[pl.ds(h, 1), :] * (
            grad_query - query * jnp.sum(grad_query * query, axis=0, keepdims=True)
        )
        grad_key = unit_scale_ref[pl.ds(h + HEADS, 1), :] * (
            grad_key - key * jnp.sum(grad_key * key, axis=0, keepdims=True)
        )
        grad_query_ref[out_rows, :] = grad_query.astype(BF)
        grad_key_ref[out_rows, :] = grad_key.astype(BF)
        return carry

    lax.fori_loop(0, count, scores, 0, unroll=8)
    lax.fori_loop(0, count, units, 0, unroll=16)


def input_kernel(*refs):
    parts, w_qkv_ref, out_refs = refs[:-5], refs[-5], refs[-4:]
    for row in range(0, C, TOK):
        total, col = 0.0, 0
        for part in parts:
            size = part.shape[0]
            total += dot(w_qkv_ref[row : row + TOK, col : col + size], part[...])
            col += size
        total = total.T.astype(BF)
        for n, out_ref in enumerate(out_refs):
            out_ref[:, row : row + TOK] = total[n * 64 : n * 64 + 64]


VM = pl.BlockSpec(memory_space=pltpu.VMEM)
ANY = pl.BlockSpec(memory_space=pl.ANY)
SM = pl.BlockSpec(memory_space=pltpu.SMEM)


def shape(dims, kind):
    return jax.ShapeDtypeStruct(dims, kind)


def call(kernel, outs, ins, micros, name, limit, scratch=()):
    return pl.pallas_call(
        kernel,
        out_shape=outs,
        in_specs=ins,
        out_specs=jax.tree.map(lambda _: VM, outs),
        scratch_shapes=scratch,
        compiler_params=pltpu.CompilerParams(vmem_limit_bytes=limit * MIB),
        cost_estimate=pl.CostEstimate(
            flops=int(micros * 11 * 10**8), bytes_accessed=MIB, transcendentals=0
        ),
        name=name,
    )


def project(quads, w_qkv, after):
    flat = shape((C, TOK), F32)
    outs = (
        flat, flat, shape((C, TOK), BF), shape((2 * HEADS, TOK), F32), shape((TOK, C), BF),
    )
    scratch = [pltpu.VMEM((C, 3 * C), BF), pltpu.SemaphoreType.DMA((3,))]
    ins = [VM] * 4 + [pl.BlockSpec(memory_space=pltpu.HBM), ANY]
    return call(project_kernel, outs, ins, 4, "project_part", 24, scratch)(
        *quads, pltpu.with_memory_space_constraint(w_qkv, pltpu.HBM), after
    )


def attention(rows, cols, *args):
    outs = (shape((C, TOK), BF), shape((HEADS, TOK, TOK), F32))
    kernel = functools.partial(attention_kernel, rows, cols)
    return call(kernel, outs, [VM] * 3 + [SM] + [ANY] * 3, 6, "attention_part", 16)(*args)


def output_norm(att, quads, w_proj, gain, after):
    outs = (shape((TOK, C), BF), shape((C, TOK), BF))
    return call(norm_kernel, outs, [VM] * 7 + [ANY], 2, "norm_part", 16)(
        att, *quads, w_proj, gain, after
    )


def value_grads(*args):
    ins = [VM] * 2 + [ANY]
    return call(value_kernel, shape((C, TOK), BF), ins, 2, "value_part", 16)(*args)


def left_rows(*args):
    ins = [VM] * 5 + [ANY]
    return call(left_kernel, shape((C, 2 * TOK), BF), ins, 1.2, "left_rows", 24)(*args)


def weight_terms(*args):
    def part(*spans):
        outs = (shape((TOK, C), BF),) * (sum(b - a for a, b in spans) // TOK)
        kernel = functools.partial(term_kernel, spans)
        return call(kernel, outs, [VM] * 5, 0.6, "weight_terms", 24)(*args)

    (far,) = part((2 * TOK, 3 * TOK))
    own, one, three = part((0, 2 * TOK), (3 * TOK, 4 * TOK))
    return own, one, far, three


def score_grads(first, count, *args):
    outs = (shape((count * DIM, TOK), BF),) * 2
    scratch = [pltpu.VMEM((count, TOK, TOK), BF)]
    kernel = functools.partial(score_kernel, first, count)
    ins = [VM] * 6 + [SM, ANY]
    return call(kernel, outs, ins, 0.3, "score_part", 16, scratch)(*args)


def block_sums(count, *blocks):
    outs = (shape((64, C), BF),) * count
    return call(sum_kernel, outs, [VM] * 4, 0.5, "block_sums", 16)(*blocks)


def input_grad(parts, w_qkv):
    outs = (shape((TOK // 4, C), BF),) * 4
    return call(input_kernel, outs, [VM] * (len(parts) + 1), 0.2, "input_part", 24)(*parts, w_qkv)


def passed(array, d_row, d_col, rows, cols):
    pairs = [
        (r * cols + c, (r + d_row) % rows * cols + (c + d_col) % cols)
        for r in range(rows)
        for c in range(cols)
    ]
    return lax.ppermute(array, ("row", "col"), pairs)


def window(array, rows, cols):
    def quad(r, c):
        return array[r : r + HALF, c : c + HALF].reshape(TOK // 4, C)

    return (
        quad(HALF, HALF),
        passed(quad(HALF, 0), 0, -1, rows, cols),
        passed(quad(0, HALF), -1, 0, rows, cols),
        passed(quad(0, 0), -1, -1, rows, cols),
    )


def line(x, y, z, core):
    return ((z * 2 + x // 2) * 2 + core) * 8 + y * 2 + x % 2


CHIPS = [(x, y, z, core) for x in range(4) for y in range(4) for z in range(8) for core in range(2)]
BOTH = ("row", "col")


def other_core(array):
    pairs = [(line(x, y, z, core), line(x, y, z, 1 - core)) for x, y, z, core in CHIPS]
    return lax.ppermute(array, BOTH, pairs)


def moved(array, stage, by):
    pairs = []
    for x, y, z, core in CHIPS:
        to = ((x + by) % 4, y) if core == stage else (x, (y + by) % 4)
        pairs.append((line(x, y, z, core), line(*to, z, core)))
    return lax.ppermute(array, BOTH, pairs)


def gathered(blocks, stage):
    far = moved(blocks[2], stage, 2)
    return far, moved(blocks[1], stage, 1), moved(blocks[3], stage, -1)


def row_order():
    place = jnp.arange(C, dtype=jnp.int32)
    a, b, z, far, row = place // 256, place // 64 % 4, place // 8 % 8, place // 4 % 2, place % 4
    r, c = lax.axis_index("row"), lax.axis_index("col")
    core = r % 2
    dx, dy = jnp.where(core == 0, a, b), jnp.where(core == 0, b, a)
    x = (r // 2 % 2 * 2 + c % 2 + dx) % 4
    y = (c // 2 + dy) % 4
    source = z * 128 + x // 2 * 64 + far * 32 + y * 8 + x % 2 * 4 + row
    return (source[:, None] == jnp.arange(C, dtype=jnp.int32)[None, :]).astype(BF)


def group_sum(blocks, groups):
    got = lax.all_to_all(blocks, BOTH, 0, 0, axis_index_groups=groups, tiled=True)
    return jnp.sum(got.astype(F32), axis=0)


def chip_column_sum(blocks):
    groups = [
        [line(x, y, z, core) for z in range(8) for core in range(2)]
        for x in range(4)
        for y in range(4)
    ]
    got = lax.all_to_all(blocks, BOTH, 0, 0, axis_index_groups=groups, tiled=True)
    got = jnp.sum(got.reshape(8, 2, 4, C).astype(F32), axis=0)
    return got[0], got[1]


def per_device(tokens, grad_out, w_qkv, w_proj, norm_gain, logit_scale):
    rows, cols = lax.axis_size("row"), lax.axis_size("col")
    x = window(tokens, rows, cols)
    g = window(grad_out, rows, cols)
    order = row_order()
    query, key, value, unit_scale, tokens_win = project(x, w_qkv, order)
    att, probs = attention(rows, cols, query, key, value, logit_scale, *g[1:])
    tokens_win2, att2 = other_core(tokens_win), other_core(att)
    grad_mix, grad_att = output_norm(att, g, w_proj, norm_gain.reshape(1, C), tokens_win2)
    grad_value = value_grads(probs, grad_att, att2)
    grad_mix2, grad_value2 = other_core(grad_mix), other_core(grad_value)
    left = left_rows(order, att, att2, tokens_win, tokens_win2, grad_value)
    blocks = weight_terms(left, grad_mix, grad_mix2, grad_value, grad_value2)
    others = gathered(blocks, 0)
    grads = score_grads(
        0, HEADS, probs, grad_att, query, key, value, unit_scale, logit_scale, blocks[0]
    )
    parts = [*grads, grad_value]
    grad_input = input_grad(parts, w_qkv)
    grad_input, others = lax.optimization_barrier((grad_input, others))
    blocks = block_sums(4, blocks[0], *others)
    blocks, grad_input = lax.optimization_barrier((blocks, grad_input))
    others = gathered(blocks, 1)
    (terms,) = block_sums(1, blocks[0], *others)
    proj_part, value_part = chip_column_sum(terms.reshape(16, 4, C))
    back = jnp.stack(
        [
            passed(grad_input[3], 1, 1, rows, cols),
            passed(grad_input[2], 1, 0, rows, cols),
            passed(grad_input[1], 0, 1, rows, cols),
            grad_input[0],
        ]
    )
    back = back.reshape(2, 2, HALF, HALF, C).transpose(0, 2, 1, 3, 4).reshape(WIN, WIN, C)
    grad_tokens = (grad_out.astype(F32) + back.astype(F32)).astype(BF)
    return (grad_tokens, value_part, proj_part)


def solution(mesh):
    in_specs = (P("row", "col", None), P("row", "col", None), P(), P(), P(), P())
    out_specs = (P("row", "col", None), P(("row", "col"), None), P(("row", "col"), None))
    return jax.shard_map(
        per_device, mesh=mesh, in_specs=in_specs, out_specs=out_specs, check_vma=False
    )
```

```python
import functools
import math

import jax
import jax.numpy as jnp
from jax import lax
from jax.experimental import pallas as pl
from jax.experimental.pallas import tpu as pltpu
from jax.sharding import PartitionSpec as P

HEADS = 32
WIN = 16
HALF = WIN // 2
DIM = 32
TOK = WIN * WIN
C = 1024
EPS_NORM = 1e-06
EPS_LN = 1e-05
LOG2E = math.log2(math.e)
BLOCK = 2.0**20
BF = jnp.bfloat16
F32 = jnp.float32
MIB = 2**20


def dot(left, right, dims=((1,), (0,))):
    return lax.dot_general(left, right, (dims, ((), ())), preferred_element_type=F32)


TN = ((0,), (0,))
NT = ((1,), (1,))
TT = ((0,), (1,))


def head_rows(h):
    return pl.ds(pl.multiple_of(h * DIM, DIM), DIM)


def core_index():
    return lax.rem(lax.axis_index("row"), 2)


def last_window(rows, cols):
    last_row = (lax.axis_index("row") == rows - 1).astype(F32)
    last_col = (lax.axis_index("col") == cols - 1).astype(F32)
    return last_row, last_col


def mask_features(last_row, last_col):
    feature = lax.broadcasted_iota(jnp.int32, (16, TOK), 0)
    token = lax.broadcasted_iota(jnp.int32, (16, TOK), 1)
    low = (token // (TOK // 2)).astype(F32)
    far = (token // (TOK // 4) % 2).astype(F32)

    def rows(*values):
        out = jnp.zeros((16, TOK), F32)
        for n, value in enumerate(values):
            out = jnp.where(feature == n, value, out)
        return out

    key = rows(low, 1 - low, far, 1 - far)
    query = -BLOCK * rows(
        last_row * (1 - low), last_row * low, last_col * (1 - far), last_col * far
    )
    return key.astype(BF), query.astype(BF)


def project_kernel(
    x0_ref, x1_ref, x2_ref, x3_ref, w_hbm_ref, after_ref,
    query_ref, key_ref, value_ref, unit_scale_ref, window_ref, w_qkv_ref, sems,
):
    copies = []
    for n in range(3):
        span = pl.ds(n * C, C)
        copies.append(
            pltpu.make_async_copy(w_hbm_ref.at[:, span], w_qkv_ref.at[:, span], sems.at[n])
        )
        copies[-1].start()
    x = jnp.concatenate([x0_ref[...], x1_ref[...], x2_ref[...], x3_ref[...]], axis=0)
    window_ref[...] = x
    for col in range(0, 3 * C, TOK):
        if col % C == 0:
            copies[col // C].wait()
        raw = dot(x, w_qkv_ref[:, col : col + TOK]).T
        if col < 2 * C:
            heads = raw.reshape(TOK // DIM, DIM, TOK)
            inv = lax.rsqrt(jnp.sum(heads * heads, axis=1, keepdims=True) + EPS_NORM)
            unit = (heads * inv).reshape(TOK, TOK)
            unit_scale_ref[col // DIM : (col + TOK) // DIM, :] = inv[:, 0, :]
            if col < C:
                query_ref[col : col + TOK, :] = unit
            else:
                key_ref[col - C : col - C + TOK, :] = unit
        else:
            value_ref[col - 2 * C : col - 2 * C + TOK, :] = raw.astype(BF)


def attention_kernel(
    rows, cols, query_ref, key_ref, value_ref, scale_ref, after_ref, after2_ref, after3_ref,
    att_ref, probs_ref,
):
    key_mask, query_mask = mask_features(*last_window(rows, cols))

    def head(h, carry):
        rows = head_rows(h)
        raw = dot(
            jnp.concatenate([key_ref[rows, :].astype(BF), key_mask], axis=0),
            jnp.concatenate([query_ref[rows, :].astype(BF), query_mask], axis=0),
            TN,
        )
        top = jnp.max(raw, axis=0, keepdims=True)
        expo = jnp.exp2((raw - top) * (scale_ref[h] * LOG2E))
        probs = expo * (1.0 / jnp.sum(expo, axis=0, keepdims=True))
        probs_ref[h] = probs
        att_ref[rows, :] = dot(probs.astype(BF), value_ref[rows, :], TT).T.astype(BF)
        return carry

    lax.fori_loop(0, HEADS, head, 0, unroll=HEADS)


def norm_kernel(
    att_ref, g0_ref, g1_ref, g2_ref, g3_ref, w_proj_ref, gain_ref, after_ref,
    grad_mix_ref, grad_att_ref,
):
    g = jnp.concatenate([g0_ref[...], g1_ref[...], g2_ref[...], g3_ref[...]], axis=0)
    mixed = dot(att_ref[...], w_proj_ref[...], TN)
    center = mixed - jnp.mean(mixed, axis=-1, keepdims=True)
    inv_std = lax.rsqrt(jnp.mean(center * center, axis=-1, keepdims=True) + EPS_LN)
    normed = center * inv_std
    grad_norm = g.astype(F32) * gain_ref[...]
    grad_mix = inv_std * (
        grad_norm
        - jnp.mean(grad_norm, axis=-1, keepdims=True)
        - normed * jnp.mean(grad_norm * normed, axis=-1, keepdims=True)
    )
    grad_mix = grad_mix.astype(BF)
    grad_mix_ref[...] = grad_mix
    for row in range(0, C, TOK):
        grad_att_ref[row : row + TOK, :] = dot(
            w_proj_ref[row : row + TOK, :], grad_mix, NT
        ).astype(BF)


def value_kernel(probs_ref, grad_att_ref, after_ref, after2_ref, grad_value_ref):
    def head(h, carry):
        rows = head_rows(h)
        grad_value_ref[rows, :] = dot(
            grad_att_ref[rows, :], probs_ref[h].astype(BF), NT
        ).astype(BF)
        return carry

    lax.fori_loop(0, HEADS, head, 0, unroll=HEADS)


def left_kernel(order_ref, att_ref, att2_ref, x_ref, x2_ref, after_ref, left_ref):
    @pl.when(core_index() == 0)
    def _():
        att = jnp.concatenate([att_ref[...], att2_ref[...]], axis=1)
        left_ref[...] = dot(order_ref[...], att).astype(BF)

    @pl.when(core_index() == 1)
    def _():
        x = jnp.concatenate([x_ref[...], x2_ref[...]], axis=0)
        left_ref[...] = dot(order_ref[...], x, NT).astype(BF)


def term_kernel(
    spans, left_ref, grad_mix_ref, grad_mix2_ref, grad_value_ref, grad_value2_ref, *out_refs
):
    def write(col, term):
        for n, out_ref in enumerate(out_refs):
            out_ref[:, col : col + TOK] = term[n * TOK : n * TOK + TOK].astype(BF)

    left = jnp.concatenate([left_ref[a:b, :] for a, b in spans], axis=0)

    @pl.when(core_index() == 0)
    def _():
        grad_mix = jnp.concatenate([grad_mix_ref[...], grad_mix2_ref[...]], axis=0)
        for col in range(0, C, TOK):
            write(col, dot(left, grad_mix[:, col : col + TOK]))

    @pl.when(core_index() == 1)
    def _():
        grad_value = jnp.concatenate([grad_value_ref[...], grad_value2_ref[...]], axis=1)
        for col in range(0, C, TOK):
            write(col, dot(left, grad_value[col : col + TOK, :], NT))


def sum_kernel(own_ref, *refs):
    total = own_ref[...].astype(F32)
    for other in refs[:3]:
        total += other[...].astype(F32)
    total = total.astype(BF)
    size = total.shape[0] // len(refs[3:])
    for n, out_ref in enumerate(refs[3:]):
        out_ref[...] = total[n * size : n * size + size]


def score_kernel(
    first, count, probs_ref, grad_att_ref, query_ref, key_ref, value_ref, unit_scale_ref,
    scale_ref, after_ref, grad_query_ref, grad_key_ref, grad_score_ref,
):
    def scores(n, carry):
        h = n + first
        rows = head_rows(h)
        probs = probs_ref[h]
        grad_prob = dot(value_ref[rows, :], grad_att_ref[rows, :], TN)
        mean = jnp.sum(grad_prob * probs, axis=0, keepdims=True)
        grad_score_ref[n] = (scale_ref[h] * (probs * (grad_prob - mean))).astype(BF)
        return carry

    def units(n, carry):
        h = n + first
        rows, out_rows = head_rows(h), head_rows(n)
        query = query_ref[rows, :]
        key = key_ref[rows, :]
        grad_score = grad_score_ref[n]
        grad_query = dot(key.astype(BF), grad_score)
        grad_key = dot(grad_score, query.astype(BF), NT).T
        grad_query = unit_scale_ref[pl.ds(h, 1), :] * (
            grad_query - query * jnp.sum(grad_query * query, axis=0, keepdims=True)
        )
        grad_key = unit_scale_ref[pl.ds(h + HEADS, 1), :] * (
            grad_key - key * jnp.sum(grad_key * key, axis=0, keepdims=True)
        )
        grad_query_ref[out_rows, :] = grad_query.astype(BF)
        grad_key_ref[out_rows, :] = grad_key.astype(BF)
        return carry

    lax.fori_loop(0, count, scores, 0, unroll=8)
    lax.fori_loop(0, count, units, 0, unroll=16)


def input_kernel(*refs):
    parts, w_qkv_ref, out_refs = refs[:-5], refs[-5], refs[-4:]
    for row in range(0, C, TOK):
        total, col = 0.0, 0
        for part in parts:
            size = part.shape[0]
            total += dot(w_qkv_ref[row : row + TOK, col : col + size], part[...])
            col += size
        total = total.T.astype(BF)
        for n, out_ref in enumerate(out_refs):
            out_ref[:, row : row + TOK] = total[n * 64 : n * 64 + 64]


VM = pl.BlockSpec(memory_space=pltpu.VMEM)
ANY = pl.BlockSpec(memory_space=pl.ANY)
SM = pl.BlockSpec(memory_space=pltpu.SMEM)


def shape(dims, kind):
    return jax.ShapeDtypeStruct(dims, kind)


def call(kernel, outs, ins, micros, name, limit, scratch=()):
    return pl.pallas_call(
        kernel,
        out_shape=outs,
        in_specs=ins,
        out_specs=jax.tree.map(lambda _: VM, outs),
        scratch_shapes=scratch,
        compiler_params=pltpu.CompilerParams(vmem_limit_bytes=limit * MIB),
        cost_estimate=pl.CostEstimate(
            flops=int(micros * 11 * 10**8), bytes_accessed=MIB, transcendentals=0
        ),
        name=name,
    )


def project(quads, w_qkv, after):
    flat = shape((C, TOK), F32)
    outs = (
        flat, flat, shape((C, TOK), BF), shape((2 * HEADS, TOK), F32), shape((TOK, C), BF),
    )
    scratch = [pltpu.VMEM((C, 3 * C), BF), pltpu.SemaphoreType.DMA((3,))]
    ins = [VM] * 4 + [pl.BlockSpec(memory_space=pltpu.HBM), ANY]
    return call(project_kernel, outs, ins, 4, "project_part", 24, scratch)(
        *quads, pltpu.with_memory_space_constraint(w_qkv, pltpu.HBM), after
    )


def attention(rows, cols, *args):
    outs = (shape((C, TOK), BF), shape((HEADS, TOK, TOK), F32))
    kernel = functools.partial(attention_kernel, rows, cols)
    return call(kernel, outs, [VM] * 3 + [SM] + [ANY] * 3, 6, "attention_part", 16)(*args)


def output_norm(att, quads, w_proj, gain, after):
    outs = (shape((TOK, C), BF), shape((C, TOK), BF))
    return call(norm_kernel, outs, [VM] * 7 + [ANY], 2, "norm_part", 16)(
        att, *quads, w_proj, gain, after
    )


def value_grads(*args):
    ins = [VM] * 2 + [ANY] * 2
    return call(value_kernel, shape((C, TOK), BF), ins, 2, "value_part", 16)(*args)


def left_rows(*args):
    ins = [VM] * 5 + [ANY]
    return call(left_kernel, shape((C, 2 * TOK), BF), ins, 1.2, "left_rows", 24)(*args)


def weight_terms(*args):
    def part(*spans):
        outs = (shape((TOK, C), BF),) * (sum(b - a for a, b in spans) // TOK)
        kernel = functools.partial(term_kernel, spans)
        return call(kernel, outs, [VM] * 5, 0.6, "weight_terms", 24)(*args)

    (far,) = part((2 * TOK, 3 * TOK))
    own, one, three = part((0, 2 * TOK), (3 * TOK, 4 * TOK))
    return own, one, far, three


def score_grads(first, count, *args):
    outs = (shape((count * DIM, TOK), BF),) * 2
    scratch = [pltpu.VMEM((count, TOK, TOK), BF)]
    kernel = functools.partial(score_kernel, first, count)
    ins = [VM] * 6 + [SM, ANY]
    return call(kernel, outs, ins, 0.3, "score_part", 16, scratch)(*args)


def block_sums(count, *blocks):
    outs = (shape((64, C), BF),) * count
    return call(sum_kernel, outs, [VM] * 4, 0.5, "block_sums", 16)(*blocks)


def input_grad(parts, w_qkv):
    outs = (shape((TOK // 4, C), BF),) * 4
    return call(input_kernel, outs, [VM] * (len(parts) + 1), 0.2, "input_part", 24)(*parts, w_qkv)


def passed(array, d_row, d_col, rows, cols):
    pairs = [
        (r * cols + c, (r + d_row) % rows * cols + (c + d_col) % cols)
        for r in range(rows)
        for c in range(cols)
    ]
    return lax.ppermute(array, ("row", "col"), pairs)


def window(array, rows, cols):
    def quad(r, c):
        return array[r : r + HALF, c : c + HALF].reshape(TOK // 4, C)

    return (
        quad(HALF, HALF),
        passed(quad(HALF, 0), 0, -1, rows, cols),
        passed(quad(0, HALF), -1, 0, rows, cols),
        passed(quad(0, 0), -1, -1, rows, cols),
    )


def line(x, y, z, core):
    return ((z * 2 + x // 2) * 2 + core) * 8 + y * 2 + x % 2


CHIPS = [(x, y, z, core) for x in range(4) for y in range(4) for z in range(8) for core in range(2)]
BOTH = ("row", "col")


def other_core(array):
    pairs = [(line(x, y, z, core), line(x, y, z, 1 - core)) for x, y, z, core in CHIPS]
    return lax.ppermute(array, BOTH, pairs)


def moved(array, stage, by):
    pairs = []
    for x, y, z, core in CHIPS:
        to = ((x + by) % 4, y) if core == stage else (x, (y + by) % 4)
        pairs.append((line(x, y, z, core), line(*to, z, core)))
    return lax.ppermute(array, BOTH, pairs)


def gathered(blocks, stage):
    far = moved(blocks[2], stage, 2)
    return far, moved(blocks[1], stage, 1), moved(blocks[3], stage, -1)


def row_order():
    place = jnp.arange(C, dtype=jnp.int32)
    a, b, z, far, row = place // 256, place // 64 % 4, place // 8 % 8, place // 4 % 2, place % 4
    r, c = lax.axis_index("row"), lax.axis_index("col")
    core = r % 2
    dx, dy = jnp.where(core == 0, a, b), jnp.where(core == 0, b, a)
    x = (r // 2 % 2 * 2 + c % 2 + dx) % 4
    y = (c // 2 + dy) % 4
    source = z * 128 + x // 2 * 64 + far * 32 + y * 8 + x % 2 * 4 + row
    return (source[:, None] == jnp.arange(C, dtype=jnp.int32)[None, :]).astype(BF)


def group_sum(blocks, groups):
    got = lax.all_to_all(blocks, BOTH, 0, 0, axis_index_groups=groups, tiled=True)
    return jnp.sum(got.astype(F32), axis=0)


def chip_column_sum(blocks):
    groups = [
        [line(x, y, z, core) for z in range(8) for core in range(2)]
        for x in range(4)
        for y in range(4)
    ]
    got = lax.all_to_all(blocks, BOTH, 0, 0, axis_index_groups=groups, tiled=True)
    got = jnp.sum(got.reshape(8, 2, 4, C).astype(F32), axis=0)
    return got[0], got[1]


def per_device(tokens, grad_out, w_qkv, w_proj, norm_gain, logit_scale):
    rows, cols = lax.axis_size("row"), lax.axis_size("col")
    x = window(tokens, rows, cols)
    g = window(grad_out, rows, cols)
    order = row_order()
    query, key, value, unit_scale, tokens_win = project(x, w_qkv, order)
    att, probs = attention(rows, cols, query, key, value, logit_scale, *g[1:])
    tokens_win2, att2 = other_core(tokens_win), other_core(att)
    grad_mix, grad_att = output_norm(att, g, w_proj, norm_gain.reshape(1, C), tokens_win)
    grad_value = value_grads(probs, grad_att, att2, tokens_win2)
    grad_mix2, grad_value2 = other_core(grad_mix), other_core(grad_value)
    left = left_rows(order, att, att2, tokens_win, tokens_win2, grad_value)
    blocks = weight_terms(left, grad_mix, grad_mix2, grad_value, grad_value2)
    others = gathered(blocks, 0)
    grads = score_grads(
        0, HEADS, probs, grad_att, query, key, value, unit_scale, logit_scale, blocks[0]
    )
    parts = [*grads, grad_value]
    grad_input = input_grad(parts, w_qkv)
    grad_input, others = lax.optimization_barrier((grad_input, others))
    blocks = block_sums(4, blocks[0], *others)
    blocks, grad_input = lax.optimization_barrier((blocks, grad_input))
    others = gathered(blocks, 1)
    (terms,) = block_sums(1, blocks[0], *others)
    proj_part, value_part = chip_column_sum(terms.reshape(16, 4, C))
    back = jnp.stack(
        [
            passed(grad_input[3], 1, 1, rows, cols),
            passed(grad_input[2], 1, 0, rows, cols),
            passed(grad_input[1], 0, 1, rows, cols),
            grad_input[0],
        ]
    )
    back = back.reshape(2, 2, HALF, HALF, C).transpose(0, 2, 1, 3, 4).reshape(WIN, WIN, C)
    grad_tokens = (grad_out.astype(F32) + back.astype(F32)).astype(BF)
    return (grad_tokens, value_part, proj_part)


def solution(mesh):
    in_specs = (P("row", "col", None), P("row", "col", None), P(), P(), P(), P())
    out_specs = (P("row", "col", None), P(("row", "col"), None), P(("row", "col"), None))
    return jax.shard_map(
        per_device, mesh=mesh, in_specs=in_specs, out_specs=out_specs, check_vma=False
    )
```
